32 devices in a mesh: tm: 16 (over z, y, x), dp: 2 (over core).
Axes of the slice: x: 2, y: 2, z: 4, core: 2. Of those that a mesh axis runs over, the one named last changes fastest.
Arguments:
- movie: bfloat16 [2, 64, 8, 16, 128], P('dp', 'tm'), may hold values from -6 to 6
- kernel_one: bfloat16 [3456, 128], replicated, may hold values from -0.15625 to 0.15625
- kernel_two: bfloat16 [3456, 128], replicated, may hold values from -0.15625 to 0.15625
- upstream: bfloat16 [2, 64, 8, 16, 128], P('dp', 'tm'), may hold values from -6 to 6
Outputs:
- output: bfloat16 [2, 64, 8, 16, 128], P('dp', 'tm')
- movie_grad: bfloat16 [2, 64, 8, 16, 128], P('dp', 'tm')
- grad_one: float32 [3456, 128], P('tm')
- grad_two: float32 [3456, 128], P('tm')
The draws below stay inside these ranges and needn't reach their ends.
All inputs are finite; a program needn't handle non-finite values.
Results may differ from the reference program's by a relative error of at most 0.0053.
Values may be sent and summed in bfloat16 or wider, within the bound.
No kernel may reach another device: no remote copies, remote signals or barrier semaphores. Data moves between devices by JAX's collectives and lax.ppermute only.
A program may use at most 64 MiB of HBM per device.

```python
import jax
import jax.numpy as jnp
from jax import lax

C = 128
HH = 8
WW = 16
BATCH = 2
FRAMES = 64
KROWS = 3456


def block_levels(rng, dims, cuts, low, largest):
    loudness = 1.0
    for position, blocks in cuts:
        steps = jax.random.uniform(jax.random.fold_in(jax.random.fold_in(rng, 6), position), (blocks,), jnp.float32, low / len(cuts), largest / len(cuts))
        loudness = loudness * jnp.repeat(jnp.exp(steps), dims[position] // blocks).reshape((-1,) + (1,) * (len(dims) - 1 - position))
    return loudness


def normal_values(stream_key, extent, spread, reach, pieces=(), kind=jnp.bfloat16):
    values = spread * jax.random.normal(stream_key, extent, jnp.float32)
    if pieces:
        values = values * block_levels(stream_key, extent, pieces, -0.22, 0.18)
    return jnp.clip(values, -reach, reach).astype(kind)


def setup_inputs(seed: int = 0) -> dict:
    splits = jax.random.split(jax.random.key(seed), 5)
    movie = normal_values(splits[0], (BATCH, FRAMES, HH, WW, C), 1.0, 6.0, ((0, 2), (1, 16)))
    kernel_one = normal_values(splits[1], (KROWS, C), (KROWS // 2) ** -0.5, 0.15625)
    kernel_two = normal_values(splits[2], (KROWS, C), (KROWS // 2) ** -0.5, 0.15625)
    upstream = normal_values(splits[3], (BATCH, FRAMES, HH, WW, C), 1.0, 6.0, ((0, 2), (1, 16)))
    return {"movie": movie, "kernel_one": kernel_one, "kernel_two": kernel_two, "upstream": upstream}


def silu_grad(v):
    sig = jax.nn.sigmoid(v)
    return sig * (1.0 + v * (1.0 - sig))

def conv_full(field, kernel):
    chans = kernel.shape[1]
    weights = kernel.astype(jnp.float32).reshape(3, 3, 3, chans, chans)
    return lax.conv_general_dilated(field.astype(jnp.float32), weights, (1, 1, 1), ((2, 0), (1, 1), (1, 1)), dimension_numbers=('NDHWC', 'DHWIO', 'NDHWC'), precision=lax.Precision.HIGHEST)

def conv_back(field, kernel):
    chans = kernel.shape[1]
    weights = kernel.astype(jnp.float32).reshape(3, 3, 3, chans, chans)[::-1, ::-1, ::-1].swapaxes(3, 4)
    return lax.conv_general_dilated(field.astype(jnp.float32), weights, (1, 1, 1), ((0, 2), (1, 1), (1, 1)), dimension_numbers=('NDHWC', 'DHWIO', 'NDHWC'), precision=lax.Precision.HIGHEST)

def kernel_grad(field, grads):
    frames, height, width = (grads.shape[1], grads.shape[2], grads.shape[3])
    padded = jnp.pad(field.astype(jnp.float32), ((0, 0), (2, 0), (1, 1), (1, 1), (0, 0)))
    flat_grad = grads.astype(jnp.float32).reshape(-1, grads.shape[4])
    blocks = []
    for offset_t in range(3):
        for offset_i in range(3):
            for offset_j in range(3):
                piece = padded[:, offset_t:offset_t + frames, offset_i:offset_i + height, offset_j:offset_j + width]
                piece = piece.reshape(-1, piece.shape[4])
                blocks.append(jnp.dot(piece.T, flat_grad, precision=lax.Precision.HIGHEST))
    return jnp.concatenate(blocks, axis=0)

def reference(movie, kernel_one, kernel_two, upstream):
    movie_f = movie.astype(jnp.float32)
    act_in = jax.nn.silu(movie_f).astype(jnp.bfloat16)
    pre = conv_full(act_in, kernel_one)
    act_mid = jax.nn.silu(pre).astype(jnp.bfloat16)
    output = (movie_f + conv_full(act_mid, kernel_two)).astype(jnp.bfloat16)
    mid_grad = conv_back(upstream, kernel_two)
    pre_grad = (mid_grad * silu_grad(pre)).astype(jnp.bfloat16)
    grad_two = kernel_grad(act_mid, upstream)
    grad_one = kernel_grad(act_in, pre_grad)
    in_grad = conv_back(pre_grad, kernel_one)
    movie_grad = (upstream.astype(jnp.float32) + in_grad * silu_grad(movie_f)).astype(jnp.bfloat16)
    return (output, movie_grad, grad_one, grad_two)
```

```python
import jax
import jax.numpy as jnp
from jax import lax
from jax.experimental import pallas as pl
from jax.experimental.pallas import tpu as pltpu
from jax.sharding import PartitionSpec as P

BF16 = jnp.bfloat16
F32 = jnp.float32
TAPS = 3


def silu_grad(value):
    sig = jax.nn.sigmoid(value)
    return sig * (1.0 + value * (1.0 - sig))


def fill(patches, first, field, width, mirrored):
    frames, cells, chans = field.shape
    rows = frames * cells
    flat = field.astype(F32).reshape(rows, chans)
    column = lax.broadcasted_iota(jnp.int32, (rows, chans), 0) % width
    before = jnp.where(column == 0, 0.0, pltpu.roll(flat, 1, 0))
    after = jnp.where(column == width - 1, 0.0, pltpu.roll(flat, rows - 1, 0))
    blocks = (after, flat, before) if mirrored else (before, flat, after)
    for k, block in enumerate(blocks):
        patches[pl.ds(first, frames), width : width + cells, k * chans : (k + 1) * chans] = (
            block.astype(BF16).reshape(frames, cells, chans)
        )
    edge = jnp.zeros((frames, width, TAPS * chans), BF16)
    patches[pl.ds(first, frames), :width, :] = edge
    patches[pl.ds(first, frames), width + cells :, :] = edge


def conv_forward(patches, kernel, frames, cells, width):
    chans = kernel.shape[1]
    left = jnp.concatenate(
        [
            patches[kt : kt + frames, ki * width : ki * width + cells, :].reshape(frames * cells, TAPS * chans)
            for kt in range(TAPS)
            for ki in range(TAPS)
        ],
        axis=1,
    )
    return jnp.dot(left, kernel[...], preferred_element_type=F32)


def conv_backward(patches, kernel, frames, cells, width):
    chans = kernel.shape[1]
    left = jnp.concatenate(
        [
            patches[
                TAPS - 1 - kt : TAPS - 1 - kt + frames,
                (TAPS - 1 - ki) * width : (TAPS - 1 - ki) * width + cells,
                :,
            ].reshape(frames * cells, TAPS * chans)
            for kt in range(TAPS)
            for ki in range(TAPS)
        ],
        axis=1,
    )
    right = jnp.concatenate([kernel[tap * chans : (tap + 1) * chans, :] for tap in range(TAPS**3)], axis=1)
    return lax.dot_general(left, right, (((1,), (1,)), ((), ())), preferred_element_type=F32)


def first_kernel(width, movie, before, upstream, after, one, two, keep, send, mid, grad, mid_tail, grad_head, patches):
    frames, cells, chans = movie.shape
    halo = TAPS - 1
    whole = jnp.concatenate([before[...], movie[...]], axis=0)
    act_in = jax.nn.silu(whole.astype(F32)).astype(BF16)
    fill(patches, 0, act_in, width, False)
    pre = conv_forward(patches, one, frames, cells, width)
    act_mid = jax.nn.silu(pre).astype(BF16).reshape(frames, cells, chans)
    mid[...] = act_mid
    mid_tail[...] = act_mid[frames - halo :]
    up_ext = jnp.concatenate([upstream[...], after[...]], axis=0)
    fill(patches, 0, up_ext, width, True)
    mid_grad = conv_backward(patches, two, frames, cells, width)
    pre_grad = (mid_grad * silu_grad(pre)).astype(BF16).reshape(frames, cells, chans)
    grad[...] = pre_grad
    grad_head[...] = pre_grad[:halo]

    def store(for_one, for_two):
        for_one[:frames] = grad[...]
        for_one[frames:] = act_in
        for_two[:frames] = mid[...]
        for_two[frames:] = up_ext

    is_even = lax.axis_index("dp") % 2 == 0

    @pl.when(is_even)
    def _():
        store(keep, send)

    @pl.when(jnp.logical_not(is_even))
    def _():
        store(send, keep)


def kernel_sums(width, own, other, acc, patches, turned):
    chans = own.shape[2]
    cells = own.shape[1]
    halo = TAPS - 1
    frames = (own.shape[0] - halo) // 2
    ext = frames + halo
    odd = lax.axis_index("dp") % 2
    for clip, source in enumerate((own, other)):
        fill(patches, clip * ext, source[pl.ds(odd * frames, ext)], width, True)
        for n in range(ext):
            block = source[(1 - odd) * frames + n]
            place = (clip * ext + n) * cells
            turned[:, place : place + cells] = block.astype(F32).T.astype(BF16)
    for kt in range(TAPS):
        l_start = (1 - odd) * kt
        r_start = odd * (halo - kt)
        left = jnp.concatenate(
            [
                turned[:, pl.ds(pl.multiple_of((clip * ext + l_start) * cells, cells), frames * cells)]
                for clip in range(2)
            ],
            axis=1,
        )
        for ki in range(TAPS):
            low = (halo - ki) * width
            right = jnp.concatenate(
                [
                    patches[pl.ds(clip * ext + r_start, frames), low : low + cells, :].reshape(
                        frames * cells, TAPS * chans
                    )
                    for clip in range(2)
                ],
                axis=0,
            )
            sums = jnp.dot(left, right, preferred_element_type=F32)
            for kj in range(TAPS):
                row = ((kt * TAPS + ki) * TAPS + kj) * chans
                acc[row : row + chans, :] = sums[:, kj * chans : (kj + 1) * chans]


def plain_sums_kernel(width, own, other, acc, patches, turned):
    kernel_sums(width, own, other, acc, patches, turned)


def relative_sums_kernel(width, distance, own, other, keep, send, acc, patches, turned):
    kernel_sums(width, own, other, acc, patches, turned)
    half, rows, _ = keep.shape
    odd = lax.axis_index("dp") % 2
    me = lax.axis_index("tm")
    for r in range(2 * half):
        far = jnp.where(odd == 1, distance[1][r], distance[0][r])
        block = jnp.bitwise_xor(me, far)
        part = acc[pl.ds(pl.multiple_of(block * rows, 8), rows), :]
        if r < half:
            keep[r] = part
        else:
            send[r - half] = part.astype(BF16)


def last_kernel(width, movie, upstream, mid_before, mid, grad, grad_after, one, two, output, movie_grad, patches):
    frames, cells, chans = movie.shape
    fill(patches, 0, jnp.concatenate([mid_before[...], mid[...]], axis=0), width, False)
    out = conv_forward(patches, two, frames, cells, width).reshape(frames, cells, chans)
    movie_f = movie[...].astype(F32)
    output[...] = (movie_f + out).astype(BF16)
    fill(patches, 0, jnp.concatenate([grad[...], grad_after[...]], axis=0), width, True)
    in_grad = conv_backward(patches, one, frames, cells, width).reshape(frames, cells, chans)
    movie_grad[...] = (upstream[...].astype(F32) + in_grad * silu_grad(movie_f)).astype(BF16)


def call(body, outs, scratch, flops, *args):
    vmem = pl.BlockSpec(memory_space=pltpu.VMEM)
    size = sum(a.size * a.dtype.itemsize for a in args) + sum(o.size * o.dtype.itemsize for o in outs)
    return pl.pallas_call(
        body,
        out_shape=outs,
        in_specs=[vmem] * len(args),
        out_specs=[vmem] * len(outs),
        scratch_shapes=scratch,
        compiler_params=pltpu.CompilerParams(vmem_limit_bytes=24 * 2**20),
        cost_estimate=pl.CostEstimate(flops=flops, bytes_accessed=size, transcendentals=0),
    )(*args)


def passed_along(block, axis, distance):
    devices = range(lax.axis_size(axis))
    route = [(i - distance, i) for i in devices if i - distance in devices]
    return lax.ppermute(block, axis, route)


def swapped(block):
    return lax.ppermute(block, "dp", [(i, i ^ 1) for i in range(lax.axis_size("dp"))])


def halving_sum(keep, send, orders):
    tm, dp = lax.axis_size("tm"), lax.axis_size("dp")
    for stage in range(len(orders[0])):
        route = [
            (t * dp + d, (t ^ (1 << orders[d % 2][stage])) * dp + d) for t in range(tm) for d in range(dp)
        ]
        got = lax.ppermute(send, ("tm", "dp"), route)
        half = keep.shape[0] // 2
        if half:
            send = (keep[half:] + got[half:].astype(F32)).astype(BF16)
            keep = keep[:half] + got[:half].astype(F32)
        else:
            keep = keep + got.astype(F32)
    return keep[0]


def body(movie, kernel_one, kernel_two, upstream):
    clips, frames, height, width, chans = movie.shape
    assert clips == 1
    tm, dp = lax.axis_size("tm"), lax.axis_size("dp")
    assert dp % 2 == 0
    cells = height * width
    halo = TAPS - 1
    ext = frames + halo
    krows = kernel_one.shape[0]
    rows = krows // tm
    shape = jax.ShapeDtypeStruct
    flat = (frames, cells, chans)
    movie_r = movie.reshape(flat)
    upstream_r = upstream.reshape(flat)
    conv_flops = 2 * frames * cells * krows * chans
    patch = pltpu.VMEM((ext, cells + 2 * width, TAPS * chans), BF16)

    before = passed_along(movie_r[frames - halo :], "tm", 1)
    after = passed_along(upstream_r[:halo], "tm", -1)
    bundle = shape((frames + ext, cells, chans), BF16)
    field = shape(flat, BF16)
    edge = shape((halo, cells, chans), BF16)
    keep, send, mid, grad, mid_tail, grad_head = call(
        lambda *refs: first_kernel(width, *refs),
        [bundle, bundle, field, field, edge, edge],
        [patch],
        2 * conv_flops,
        movie_r, before, upstream_r, after, kernel_one, kernel_two,
    )
    other = swapped(send)

    scratch = [
        pltpu.VMEM((2 * ext, cells + 2 * width, TAPS * chans), BF16),
        pltpu.VMEM((chans, 2 * ext * cells), BF16),
    ]
    if dp == 2 and tm > 1 and tm & (tm - 1) == 0 and rows % 8 == 0:
        bits = tm.bit_length() - 1
        orders = (list(range(bits)), [1, 0][:bits] + list(range(2, bits)))
        distance = [
            [sum(1 << order[s] for s in range(bits) if r >> (bits - 1 - s) & 1) for r in range(tm)]
            for order in orders
        ]
        kept, sent = call(
            lambda *refs: relative_sums_kernel(width, distance, *refs),
            [shape((tm // 2, rows, chans), F32), shape((tm // 2, rows, chans), BF16)],
            [pltpu.VMEM((krows, chans), F32)] + scratch,
            2 * conv_flops,
            keep, other,
        )
        mine = halving_sum(kept, sent, orders)
    else:
        (sums,) = call(
            lambda *refs: plain_sums_kernel(width, *refs),
            [shape((krows, chans), F32)],
            scratch,
            2 * conv_flops,
            keep, other,
        )
        mine = lax.psum_scatter(sums, "tm", scatter_dimension=0, tiled=True)
        if dp > 2:
            groups = [[d for d in range(dp) if d % 2 == parity] for parity in range(2)]
            mine = lax.psum(mine, "dp", axis_index_groups=groups)

    mid_before = passed_along(mid_tail, "tm", 1)
    grad_after = passed_along(grad_head, "tm", -1)
    output, movie_grad = call(
        lambda *refs: last_kernel(width, *refs),
        [field, field],
        [patch],
        2 * conv_flops,
        movie_r, upstream_r, mid_before, mid, grad, grad_after, kernel_one, kernel_two,
    )
    theirs = swapped(mine)
    is_even = lax.axis_index("dp") % 2 == 0
    grad_one = jnp.where(is_even, mine, theirs)
    grad_two = jnp.where(is_even, theirs, mine)
    return (output.reshape(movie.shape), movie_grad.reshape(movie.shape), grad_one, grad_two)


def solution(mesh):
    in_specs = (P("dp", "tm", None, None, None), P(), P(), P("dp", "tm", None, None, None))
    out_specs = (
        P("dp", "tm", None, None, None),
        P("dp", "tm", None, None, None),
        P("tm", None),
        P("tm", None),
    )
    return jax.shard_map(body, mesh=mesh, in_specs=in_specs, out_specs=out_specs, check_vma=False)
```

```python
import jax
import jax.numpy as jnp
from jax import lax
from jax.experimental import pallas as pl
from jax.experimental.pallas import tpu as pltpu
from jax.sharding import PartitionSpec as P

BF16 = jnp.bfloat16
F32 = jnp.float32
TAPS = 3


def silu_grad(value):
    sig = jax.nn.sigmoid(value)
    return sig * (1.0 + value * (1.0 - sig))


def fill(patches, first, field, width, mirrored):
    frames, cells, chans = field.shape
    rows = frames * cells
    flat = field.astype(F32).reshape(rows, chans)
    column = lax.broadcasted_iota(jnp.int32, (rows, chans), 0) % width
    before = jnp.where(column == 0, 0.0, pltpu.roll(flat, 1, 0))
    after = jnp.where(column == width - 1, 0.0, pltpu.roll(flat, rows - 1, 0))
    blocks = (after, flat, before) if mirrored else (before, flat, after)
    for k, block in enumerate(blocks):
        patches[pl.ds(first, frames), width : width + cells, k * chans : (k + 1) * chans] = (
            block.astype(BF16).reshape(frames, cells, chans)
        )
    edge = jnp.zeros((frames, width, TAPS * chans), BF16)
    patches[pl.ds(first, frames), :width, :] = edge
    patches[pl.ds(first, frames), width + cells :, :] = edge


def conv_forward(patches, kernel, frames, cells, width):
    chans = kernel.shape[1]
    left = jnp.concatenate(
        [
            patches[kt : kt + frames, ki * width : ki * width + cells, :].reshape(frames * cells, TAPS * chans)
            for kt in range(TAPS)
            for ki in range(TAPS)
        ],
        axis=1,
    )
    return jnp.dot(left, kernel[...], preferred_element_type=F32)


def conv_backward(patches, kernel, frames, cells, width):
    chans = kernel.shape[1]
    left = jnp.concatenate(
        [
            patches[
                TAPS - 1 - kt : TAPS - 1 - kt + frames,
                (TAPS - 1 - ki) * width : (TAPS - 1 - ki) * width + cells,
                :,
            ].reshape(frames * cells, TAPS * chans)
            for kt in range(TAPS)
            for ki in range(TAPS)
        ],
        axis=1,
    )
    right = jnp.concatenate([kernel[tap * chans : (tap + 1) * chans, :] for tap in range(TAPS**3)], axis=1)
    return lax.dot_general(left, right, (((1,), (1,)), ((), ())), preferred_element_type=F32)


def taps_forward(patches, kernel, kt, first, count, cells, width):
    chans = kernel.shape[1]
    left = jnp.concatenate(
        [
            patches[first : first + count, ki * width : ki * width + cells, :].reshape(count * cells, TAPS * chans)
            for ki in range(TAPS)
        ],
        axis=1,
    )
    rows = TAPS * TAPS * chans
    return jnp.dot(left, kernel[kt * rows : (kt + 1) * rows, :], preferred_element_type=F32)


def taps_backward(patches, kernel, kt, first, count, cells, width):
    chans = kernel.shape[1]
    left = jnp.concatenate(
        [
            patches[
                first : first + count, (TAPS - 1 - ki) * width : (TAPS - 1 - ki) * width + cells, :
            ].reshape(count * cells, TAPS * chans)
            for ki in range(TAPS)
        ],
        axis=1,
    )
    taps = range(kt * TAPS * TAPS, (kt + 1) * TAPS * TAPS)
    right = jnp.concatenate([kernel[tap * chans : (tap + 1) * chans, :] for tap in taps], axis=1)
    return lax.dot_general(left, right, (((1,), (1,)), ((), ())), preferred_element_type=F32)


def edges_kernel(movie, upstream, near, far, sems):
    frames = movie.shape[0]
    halo = near.shape[0]
    even = lax.axis_index("tm") % 2 == 0

    def run(forward, backward):
        copies = [
            pltpu.make_async_copy(movie.at[pl.ds(frames - halo, halo)], forward, sems.at[0]),
            pltpu.make_async_copy(upstream.at[pl.ds(0, halo)], backward, sems.at[1]),
        ]
        for copy in copies:
            copy.start()
        for copy in copies:
            copy.wait()

    @pl.when(even)
    def _():
        run(near, far)

    @pl.when(jnp.logical_not(even))
    def _():
        run(far, near)


def sorted_edges(near, far):
    even = lax.axis_index("tm") % 2 == 0
    return jnp.where(even, far[...], near[...]), jnp.where(even, near[...], far[...])


def inner_kernel(
    width, movie, upstream, one, two, act_in, pre_part, grad_part, act_patches, up_patches
):
    frames, cells, chans = movie.shape
    act_in[...] = jax.nn.silu(movie[...].astype(F32)).astype(BF16)
    fill(act_patches, 0, act_in[...], width, False)
    fill(up_patches, 0, upstream[...], width, True)
    pre_part[...] = taps_forward(act_patches, one, TAPS - 1, 0, frames, cells, width)
    for lag in range(1, TAPS):
        part = taps_forward(act_patches, one, TAPS - 1 - lag, 0, frames - lag, cells, width)
        pre_part[lag * cells :, :] += part
    grad_part[...] = taps_backward(up_patches, two, TAPS - 1, 0, frames, cells, width)
    for lag in range(1, TAPS):
        part = taps_backward(up_patches, two, TAPS - 1 - lag, lag, frames - lag, cells, width)
        grad_part[: (frames - lag) * cells, :] += part


def outer_kernel(
    width, near, far, act_in, upstream, pre_part, grad_part, one, two, keep, send, mid, grad, near_out, far_out, patches
):
    frames, cells, chans = act_in.shape
    halo = TAPS - 1
    before, after = sorted_edges(near, far)
    act_before = jax.nn.silu(before.astype(F32)).astype(BF16)
    fill(patches, 0, act_before, width, False)
    pres = [pre_part[t * cells : (t + 1) * cells, :] for t in range(frames)]
    for kt in range(halo):
        part = taps_forward(patches, one, kt, kt, halo - kt, cells, width)
        for t in range(halo - kt):
            pres[t] = pres[t] + part[t * cells : (t + 1) * cells]
    pre = jnp.concatenate(pres, axis=0)
    act_mid = jax.nn.silu(pre).astype(BF16).reshape(frames, cells, chans)
    mid[...] = act_mid
    fill(patches, 0, after, width, True)
    grads = [grad_part[t * cells : (t + 1) * cells, :] for t in range(frames)]
    for kt in range(halo):
        part = taps_backward(patches, two, kt, 0, halo - kt, cells, width)
        for n in range(halo - kt):
            t = frames - (halo - kt) + n
            grads[t] = grads[t] + part[n * cells : (n + 1) * cells]
    mid_grad = jnp.concatenate(grads, axis=0)
    pre_grad = (mid_grad * silu_grad(pre)).astype(BF16).reshape(frames, cells, chans)
    grad[...] = pre_grad
    even = lax.axis_index("tm") % 2 == 0
    mid_tail, grad_head = act_mid[frames - halo :], pre_grad[:halo]
    near_out[...] = jnp.where(even, mid_tail, grad_head)
    far_out[...] = jnp.where(even, grad_head, mid_tail)

    def store(for_one, for_two):
        for_one[:frames] = grad[...]
        for_one[frames : frames + halo] = act_before
        for_one[frames + halo :] = act_in[...]
        for_two[:frames] = mid[...]
        for_two[frames : 2 * frames] = upstream[...]
        for_two[2 * frames :] = after

    is_even = lax.axis_index("dp") % 2 == 0

    @pl.when(is_even)
    def _():
        store(keep, send)

    @pl.when(jnp.logical_not(is_even))
    def _():
        store(send, keep)


def kernel_sums(width, own, other, acc, patches, turned):
    chans = own.shape[2]
    cells = own.shape[1]
    halo = TAPS - 1
    frames = (own.shape[0] - halo) // 2
    ext = frames + halo
    odd = lax.axis_index("dp") % 2
    for clip, source in enumerate((own, other)):
        fill(patches, clip * ext, source[pl.ds(odd * frames, ext)], width, True)
        for n in range(ext):
            block = source[(1 - odd) * frames + n]
            place = (clip * ext + n) * cells
            turned[:, place : place + cells] = block.astype(F32).T.astype(BF16)
    for kt in range(TAPS):
        l_start = (1 - odd) * kt
        r_start = odd * (halo - kt)
        left = jnp.concatenate(
            [
                turned[:, pl.ds(pl.multiple_of((clip * ext + l_start) * cells, cells), frames * cells)]
                for clip in range(2)
            ],
            axis=1,
        )
        for ki in range(TAPS):
            low = (halo - ki) * width
            right = jnp.concatenate(
                [
                    patches[pl.ds(clip * ext + r_start, frames), low : low + cells, :].reshape(
                        frames * cells, TAPS * chans
                    )
                    for clip in range(2)
                ],
                axis=0,
            )
            sums = jnp.dot(left, right, preferred_element_type=F32)
            for kj in range(TAPS):
                row = ((kt * TAPS + ki) * TAPS + kj) * chans
                acc[row : row + chans, :] = sums[:, kj * chans : (kj + 1) * chans]


def plain_sums_kernel(width, own, other, acc, patches, turned):
    kernel_sums(width, own, other, acc, patches, turned)


def relative_sums_kernel(width, distance, own, other, keep, send, acc, patches, turned):
    kernel_sums(width, own, other, acc, patches, turned)
    half, rows, _ = keep.shape
    odd = lax.axis_index("dp") % 2
    me = lax.axis_index("tm")
    for r in range(2 * half):
        far = jnp.where(odd == 1, distance[1][r], distance[0][r])
        block = jnp.bitwise_xor(me, far)
        part = acc[pl.ds(pl.multiple_of(block * rows, 8), rows), :]
        if r < half:
            keep[r] = part
        else:
            send[r - half] = part.astype(BF16)


def last_kernel(width, movie, upstream, near, far, mid, grad, one, two, output, movie_grad, patches):
    frames, cells, chans = movie.shape
    mid_before, grad_after = sorted_edges(near, far)
    fill(patches, 0, jnp.concatenate([mid_before, mid[...]], axis=0), width, False)
    out = conv_forward(patches, two, frames, cells, width).reshape(frames, cells, chans)
    movie_f = movie[...].astype(F32)
    output[...] = (movie_f + out).astype(BF16)
    fill(patches, 0, jnp.concatenate([grad[...], grad_after], axis=0), width, True)
    in_grad = conv_backward(patches, one, frames, cells, width).reshape(frames, cells, chans)
    movie_grad[...] = (upstream[...].astype(F32) + in_grad * silu_grad(movie_f)).astype(BF16)


def call(body, outs, scratch, flops, *args, unplaced=(), limit=24):
    vmem = pl.BlockSpec(memory_space=pltpu.VMEM)
    anywhere = pl.BlockSpec(memory_space=pltpu.MemorySpace.HBM)
    size = sum(a.size * a.dtype.itemsize for a in args) + sum(o.size * o.dtype.itemsize for o in outs)
    return pl.pallas_call(
        body,
        out_shape=outs,
        in_specs=[anywhere if i in unplaced else vmem for i in range(len(args))],
        out_specs=[vmem] * len(outs),
        scratch_shapes=scratch,
        compiler_params=pltpu.CompilerParams(vmem_limit_bytes=int(limit * 2**20)),
        cost_estimate=pl.CostEstimate(flops=flops, bytes_accessed=size, transcendentals=0),
    )(*args)


def paired(block, first):
    pairs = [(i, i + 1) for i in range(first, lax.axis_size("tm") - 1, 2)]
    return lax.ppermute(block, "tm", pairs + [(j, i) for i, j in pairs])


def swapped(block):
    return lax.ppermute(block, "dp", [(i, i ^ 1) for i in range(lax.axis_size("dp"))])


def distances(orders):
    out = []
    for groups in orders:
        dist = [0]
        for group in reversed(groups):
            steps = [sum(1 << bit for n, bit in enumerate(group) if q >> n & 1) for q in range(1 << len(group))]
            dist = [step | low for step in steps for low in dist]
        out.append(dist)
    return out


def exchanged(send, steps):
    tm, dp = lax.axis_size("tm"), lax.axis_size("dp")
    route = [(t * dp + d, (t ^ steps[d % 2]) * dp + d) for t in range(tm) for d in range(dp)]
    return lax.ppermute(send, ("tm", "dp"), route)


def body(movie, kernel_one, kernel_two, upstream):
    clips, frames, height, width, chans = movie.shape
    assert clips == 1
    tm, dp = lax.axis_size("tm"), lax.axis_size("dp")
    assert dp % 2 == 0
    cells = height * width
    halo = TAPS - 1
    ext = frames + halo
    krows = kernel_one.shape[0]
    rows = krows // tm
    shape = jax.ShapeDtypeStruct
    flat = (frames, cells, chans)
    movie_r = movie.reshape(flat)
    upstream_r = upstream.reshape(flat)
    conv_flops = 2 * frames * cells * krows * chans
    patch = pltpu.VMEM((ext, cells + 2 * width, TAPS * chans), BF16)

    bundle = shape((frames + ext, cells, chans), BF16)
    field = shape(flat, BF16)
    edge = shape((halo, cells, chans), BF16)
    part = shape((frames * cells, chans), F32)
    own_patch = shape((frames, cells + 2 * width, TAPS * chans), BF16)

    near, far = call(
        edges_kernel,
        [edge, edge],
        [pltpu.SemaphoreType.DMA((2,))],
        8000000000,
        movie_r, upstream_r,
        unplaced=(0, 1),
        limit=60,
    )
    near = paired(near, 0)
    far = paired(far, 1)
    act_in, pre_part, grad_part = call(
        lambda *refs: inner_kernel(width, *refs),
        [field, part, part],
        [pltpu.VMEM(own_patch.shape, BF16)] * 2,
        3 * conv_flops // 2,
        movie_r, upstream_r, kernel_one, kernel_two,
    )
    keep, send, mid, grad, near_out, far_out = call(
        lambda *refs: outer_kernel(width, *refs),
        [bundle, bundle, field, field, edge, edge],
        [pltpu.VMEM((halo, cells + 2 * width, TAPS * chans), BF16)],
        conv_flops // 2,
        near, far, act_in, upstream_r, pre_part, grad_part, kernel_one, kernel_two,
    )
    other = swapped(send)
    near_mid = paired(near_out, 0)
    far_mid = paired(far_out, 1)

    def finish(near_mid, far_mid):
        return call(
            lambda *refs: last_kernel(width, *refs),
            [field, field],
            [patch],
            2 * conv_flops,
            movie_r, upstream_r, near_mid, far_mid, mid, grad, kernel_one, kernel_two,
        )

    scratch = [
        pltpu.VMEM((2 * ext, cells + 2 * width, TAPS * chans), BF16),
        pltpu.VMEM((chans, 2 * ext * cells), BF16),
    ]
    if dp == 2 and tm > 1 and tm & (tm - 1) == 0 and rows % 8 == 0:
        bits = tm.bit_length() - 1
        rest = [list(range(low, min(low + 2, bits))) for low in range(2, bits, 2)]
        orders = ([[0], [1]][:bits] + rest, [[1], [0]][2 - min(bits, 2) :] + rest)
        kept, sent = call(
            lambda *refs: relative_sums_kernel(width, distances(orders), *refs),
            [shape((tm // 2, rows, chans), F32), shape((tm // 2, rows, chans), BF16)],
            [pltpu.VMEM((krows, chans), F32)] + scratch,
            2 * conv_flops,
            keep, other,
        )
        sent, near_mid, far_mid = lax.optimization_barrier((sent, near_mid, far_mid))
        sends = [sent]
        for stage in range(len(orders[0])):
            steps = [distances([groups[stage : stage + 1]])[0] for groups in orders]
            gots = [
                exchanged(sends[q - 1], (steps[0][q], steps[1][q])) for q in reversed(range(1, len(steps[0])))
            ]
            if stage + 1 == len(orders[0]):
                output, movie_grad = finish(near_mid, far_mid)
                *gots, output, movie_grad = lax.optimization_barrier((*gots, output, movie_grad))
            for got in gots:
                kept = kept + got.astype(F32)
            if stage + 1 < len(orders[0]):
                parts = 1 << len(orders[0][stage + 1])
                size = kept.shape[0] // parts
                sends = [kept[q * size : (q + 1) * size].astype(BF16) for q in range(1, parts)]
                kept = kept[:size]
        mine = kept[0]
    else:
        (sums,) = call(
            lambda *refs: plain_sums_kernel(width, *refs),
            [shape((krows, chans), F32)],
            scratch,
            2 * conv_flops,
            keep, other,
        )
        output, movie_grad = finish(near_mid, far_mid)
        mine = lax.psum_scatter(sums, "tm", scatter_dimension=0, tiled=True)
        if dp > 2:
            groups = [[d for d in range(dp) if d % 2 == parity] for parity in range(2)]
            mine = lax.psum(mine, "dp", axis_index_groups=groups)
    theirs = swapped(mine)
    is_even = lax.axis_index("dp") % 2 == 0
    grad_one = jnp.where(is_even, mine, theirs)
    grad_two = jnp.where(is_even, theirs, mine)
    return (output.reshape(movie.shape), movie_grad.reshape(movie.shape), grad_one, grad_two)


def solution(mesh):
    in_specs = (P("dp", "tm", None, None, None), P(), P(), P("dp", "tm", None, None, None))
    out_specs = (
        P("dp", "tm", None, None, None),
        P("dp", "tm", None, None, None),
        P("tm", None),
        P("tm", None),
    )
    return jax.shard_map(body, mesh=mesh, in_specs=in_specs, out_specs=out_specs, check_vma=False)
```

```python
import jax
import jax.numpy as jnp
from jax import lax
from jax.experimental import pallas as pl
from jax.experimental.pallas import tpu as pltpu
from jax.sharding import PartitionSpec as P

BF16 = jnp.bfloat16
F32 = jnp.float32
TAPS = 3


def silu_grad(value):
    sig = jax.nn.sigmoid(value)
    return sig * (1.0 + value * (1.0 - sig))


def fill(patches, first, field, width, mirrored):
    frames, cells, chans = field.shape
    rows = frames * cells
    flat = field.astype(F32).reshape(rows, chans)
    column = lax.broadcasted_iota(jnp.int32, (rows, chans), 0) % width
    before = jnp.where(column == 0, 0.0, pltpu.roll(flat, 1, 0))
    after = jnp.where(column == width - 1, 0.0, pltpu.roll(flat, rows - 1, 0))
    blocks = (after, flat, before) if mirrored else (before, flat, after)
    for k, block in enumerate(blocks):
        patches[pl.ds(first, frames), width : width + cells, k * chans : (k + 1) * chans] = (
            block.astype(BF16).reshape(frames, cells, chans)
        )
    edge = jnp.zeros((frames, width, TAPS * chans), BF16)
    patches[pl.ds(first, frames), :width, :] = edge
    patches[pl.ds(first, frames), width + cells :, :] = edge


def conv_forward(patches, kernel, frames, cells, width):
    chans = kernel.shape[1]
    left = jnp.concatenate(
        [
            patches[kt : kt + frames, ki * width : ki * width + cells, :].reshape(frames * cells, TAPS * chans)
            for kt in range(TAPS)
            for ki in range(TAPS)
        ],
        axis=1,
    )
    return jnp.dot(left, kernel[...], preferred_element_type=F32)


def conv_backward(patches, kernel, frames, cells, width):
    chans = kernel.shape[1]
    left = jnp.concatenate(
        [
            patches[
                TAPS - 1 - kt : TAPS - 1 - kt + frames,
                (TAPS - 1 - ki) * width : (TAPS - 1 - ki) * width + cells,
                :,
            ].reshape(frames * cells, TAPS * chans)
            for kt in range(TAPS)
            for ki in range(TAPS)
        ],
        axis=1,
    )
    right = jnp.concatenate([kernel[tap * chans : (tap + 1) * chans, :] for tap in range(TAPS**3)], axis=1)
    return lax.dot_general(left, right, (((1,), (1,)), ((), ())), preferred_element_type=F32)


def taps_forward(patches, kernel, kt, first, count, cells, width):
    chans = kernel.shape[1]
    left = jnp.concatenate(
        [
            patches[first : first + count, ki * width : ki * width + cells, :].reshape(count * cells, TAPS * chans)
            for ki in range(TAPS)
        ],
        axis=1,
    )
    rows = TAPS * TAPS * chans
    return jnp.dot(left, kernel[kt * rows : (kt + 1) * rows, :], preferred_element_type=F32)


def taps_backward(patches, kernel, kt, first, count, cells, width):
    chans = kernel.shape[1]
    left = jnp.concatenate(
        [
            patches[
                first : first + count, (TAPS - 1 - ki) * width : (TAPS - 1 - ki) * width + cells, :
            ].reshape(count * cells, TAPS * chans)
            for ki in range(TAPS)
        ],
        axis=1,
    )
    taps = range(kt * TAPS * TAPS, (kt + 1) * TAPS * TAPS)
    right = jnp.concatenate([kernel[tap * chans : (tap + 1) * chans, :] for tap in taps], axis=1)
    return lax.dot_general(left, right, (((1,), (1,)), ((), ())), preferred_element_type=F32)


def edges_kernel(movie, upstream, near, far, sems):
    frames = movie.shape[0]
    halo = near.shape[0]
    even = lax.axis_index("tm") % 2 == 0

    def run(forward, backward):
        copies = [
            pltpu.make_async_copy(movie.at[pl.ds(frames - halo, halo)], forward, sems.at[0]),
            pltpu.make_async_copy(upstream.at[pl.ds(0, halo)], backward, sems.at[1]),
        ]
        for copy in copies:
            copy.start()
        for copy in copies:
            copy.wait()

    @pl.when(even)
    def _():
        run(near, far)

    @pl.when(jnp.logical_not(even))
    def _():
        run(far, near)


def sorted_edges(near, far):
    even = lax.axis_index("tm") % 2 == 0
    return jnp.where(even, far[...], near[...]), jnp.where(even, near[...], far[...])


def inner_kernel(
    width, movie, upstream, one, two, act_in, pre_part, grad_part, act_patches, up_patches
):
    frames, cells, chans = movie.shape
    act_in[...] = jax.nn.silu(movie[...].astype(F32)).astype(BF16)
    fill(act_patches, 0, act_in[...], width, False)
    fill(up_patches, 0, upstream[...], width, True)
    pre_part[...] = taps_forward(act_patches, one, TAPS - 1, 0, frames, cells, width)
    for lag in range(1, TAPS):
        part = taps_forward(act_patches, one, TAPS - 1 - lag, 0, frames - lag, cells, width)
        pre_part[lag * cells :, :] += part
    grad_part[...] = taps_backward(up_patches, two, TAPS - 1, 0, frames, cells, width)
    for lag in range(1, TAPS):
        part = taps_backward(up_patches, two, TAPS - 1 - lag, lag, frames - lag, cells, width)
        grad_part[: (frames - lag) * cells, :] += part


def outer_kernel(
    width, near, far, act_in, upstream, pre_part, grad_part, one, two, keep, send, mid, grad, near_out, far_out, patches
):
    frames, cells, chans = act_in.shape
    halo = TAPS - 1
    before, after = sorted_edges(near, far)
    act_before = jax.nn.silu(before.astype(F32)).astype(BF16)
    fill(patches, 0, act_before, width, False)
    pres = [pre_part[t * cells : (t + 1) * cells, :] for t in range(frames)]
    for kt in range(halo):
        part = taps_forward(patches, one, kt, kt, halo - kt, cells, width)
        for t in range(halo - kt):
            pres[t] = pres[t] + part[t * cells : (t + 1) * cells]
    pre = jnp.concatenate(pres, axis=0)
    act_mid = jax.nn.silu(pre).astype(BF16).reshape(frames, cells, chans)
    mid[...] = act_mid
    fill(patches, 0, after, width, True)
    grads = [grad_part[t * cells : (t + 1) * cells, :] for t in range(frames)]
    for kt in range(halo):
        part = taps_backward(patches, two, kt, 0, halo - kt, cells, width)
        for n in range(halo - kt):
            t = frames - (halo - kt) + n
            grads[t] = grads[t] + part[n * cells : (n + 1) * cells]
    mid_grad = jnp.concatenate(grads, axis=0)
    pre_grad = (mid_grad * silu_grad(pre)).astype(BF16).reshape(frames, cells, chans)
    grad[...] = pre_grad
    even = lax.axis_index("tm") % 2 == 0
    mid_tail, grad_head = act_mid[frames - halo :], pre_grad[:halo]
    near_out[...] = jnp.where(even, mid_tail, grad_head)
    far_out[...] = jnp.where(even, grad_head, mid_tail)

    def store(for_one, for_two):
        for_one[:frames] = grad[...]
        for_one[frames : frames + halo] = act_before
        for_one[frames + halo :] = act_in[...]
        for_two[:frames] = mid[...]
        for_two[frames : 2 * frames] = upstream[...]
        for_two[2 * frames :] = after

    is_even = lax.axis_index("dp") % 2 == 0

    @pl.when(is_even)
    def _():
        store(keep, send)

    @pl.when(jnp.logical_not(is_even))
    def _():
        store(send, keep)


def kernel_sums(width, own, other, acc, patches, turned):
    chans = own.shape[2]
    cells = own.shape[1]
    halo = TAPS - 1
    frames = (own.shape[0] - halo) // 2
    ext = frames + halo
    odd = lax.axis_index("dp") % 2
    for clip, source in enumerate((own, other)):
        fill(patches, clip * ext, source[pl.ds(odd * frames, ext)], width, True)
        for n in range(ext):
            block = source[(1 - odd) * frames + n]
            place = (clip * ext + n) * cells
            turned[:, place : place + cells] = block.astype(F32).T.astype(BF16)
    for kt in range(TAPS):
        l_start = (1 - odd) * kt
        r_start = odd * (halo - kt)
        left = jnp.concatenate(
            [
                turned[:, pl.ds(pl.multiple_of((clip * ext + l_start) * cells, cells), frames * cells)]
                for clip in range(2)
            ],
            axis=1,
        )
        for ki in range(TAPS):
            low = (halo - ki) * width
            right = jnp.concatenate(
                [
                    patches[pl.ds(clip * ext + r_start, frames), low : low + cells, :].reshape(
                        frames * cells, TAPS * chans
                    )
                    for clip in range(2)
                ],
                axis=0,
            )
            sums = jnp.dot(left, right, preferred_element_type=F32)
            for kj in range(TAPS):
                row = ((kt * TAPS + ki) * TAPS + kj) * chans
                acc[row : row + chans, :] = sums[:, kj * chans : (kj + 1) * chans]


def plain_sums_kernel(width, own, other, acc, patches, turned):
    kernel_sums(width, own, other, acc, patches, turned)


def relative_sums_kernel(width, distance, own, other, keep, send, acc, patches, turned):
    kernel_sums(width, own, other, acc, patches, turned)
    half, rows, _ = keep.shape
    odd = lax.axis_index("dp") % 2
    me = lax.axis_index("tm")
    for r in range(2 * half):
        far = jnp.where(odd == 1, distance[1][r], distance[0][r])
        block = jnp.bitwise_xor(me, far)
        part = acc[pl.ds(pl.multiple_of(block * rows, 8), rows), :]
        if r < half:
            keep[r] = part
        else:
            send[r - half] = part.astype(BF16)


def last_kernel(width, movie, upstream, near, far, mid, grad, one, two, output, movie_grad, patches):
    frames, cells, chans = movie.shape
    mid_before, grad_after = sorted_edges(near, far)
    fill(patches, 0, jnp.concatenate([mid_before, mid[...]], axis=0), width, False)
    out = conv_forward(patches, two, frames, cells, width).reshape(frames, cells, chans)
    movie_f = movie[...].astype(F32)
    output[...] = (movie_f + out).astype(BF16)
    fill(patches, 0, jnp.concatenate([grad[...], grad_after], axis=0), width, True)
    in_grad = conv_backward(patches, one, frames, cells, width).reshape(frames, cells, chans)
    movie_grad[...] = (upstream[...].astype(F32) + in_grad * silu_grad(movie_f)).astype(BF16)


def call(body, outs, scratch, flops, *args, unplaced=(), limit=24):
    vmem = pl.BlockSpec(memory_space=pltpu.VMEM)
    anywhere = pl.BlockSpec(memory_space=pltpu.MemorySpace.HBM)
    size = sum(a.size * a.dtype.itemsize for a in args) + sum(o.size * o.dtype.itemsize for o in outs)
    return pl.pallas_call(
        body,
        out_shape=outs,
        in_specs=[anywhere if i in unplaced else vmem for i in range(len(args))],
        out_specs=[vmem] * len(outs),
        scratch_shapes=scratch,
        compiler_params=pltpu.CompilerParams(vmem_limit_bytes=int(limit * 2**20)),
        cost_estimate=pl.CostEstimate(flops=flops, bytes_accessed=size, transcendentals=0),
    )(*args)


def paired(block, first):
    pairs = [(i, i + 1) for i in range(first, lax.axis_size("tm") - 1, 2)]
    return lax.ppermute(block, "tm", pairs + [(j, i) for i, j in pairs])


def swapped(block):
    return lax.ppermute(block, "dp", [(i, i ^ 1) for i in range(lax.axis_size("dp"))])


def distances(orders):
    out = []
    for groups in orders:
        dist = [0]
        for group in reversed(groups):
            steps = [sum(1 << bit for n, bit in enumerate(group) if q >> n & 1) for q in range(1 << len(group))]
            dist = [step | low for step in steps for low in dist]
        out.append(dist)
    return out


def exchanged(send, steps):
    tm, dp = lax.axis_size("tm"), lax.axis_size("dp")
    route = [(t * dp + d, (t ^ steps[d % 2]) * dp + d) for t in range(tm) for d in range(dp)]
    return lax.ppermute(send, ("tm", "dp"), route)


def body(movie, kernel_one, kernel_two, upstream):
    clips, frames, height, width, chans = movie.shape
    assert clips == 1
    tm, dp = lax.axis_size("tm"), lax.axis_size("dp")
    assert dp % 2 == 0
    cells = height * width
    halo = TAPS - 1
    ext = frames + halo
    krows = kernel_one.shape[0]
    rows = krows // tm
    shape = jax.ShapeDtypeStruct
    flat = (frames, cells, chans)
    movie_r = movie.reshape(flat)
    upstream_r = upstream.reshape(flat)
    conv_flops = 2 * frames * cells * krows * chans
    patch = pltpu.VMEM((ext, cells + 2 * width, TAPS * chans), BF16)

    bundle = shape((frames + ext, cells, chans), BF16)
    field = shape(flat, BF16)
    edge = shape((halo, cells, chans), BF16)
    part = shape((frames * cells, chans), F32)
    own_patch = shape((frames, cells + 2 * width, TAPS * chans), BF16)

    near, far = call(
        edges_kernel,
        [edge, edge],
        [pltpu.SemaphoreType.DMA((2,))],
        8000000000,
        movie_r, upstream_r,
        unplaced=(0, 1),
        limit=53.8,
    )
    near = paired(near, 0)
    far = paired(far, 1)
    act_in, pre_part, grad_part = call(
        lambda *refs: inner_kernel(width, *refs),
        [field, part, part],
        [pltpu.VMEM(own_patch.shape, BF16)] * 2,
        3 * conv_flops // 2,
        movie_r, upstream_r, kernel_one, kernel_two,
    )
    keep, send, mid, grad, near_out, far_out = call(
        lambda *refs: outer_kernel(width, *refs),
        [bundle, bundle, field, field, edge, edge],
        [pltpu.VMEM((halo, cells + 2 * width, TAPS * chans), BF16)],
        conv_flops // 2,
        near, far, act_in, upstream_r, pre_part, grad_part, kernel_one, kernel_two,
    )
    other = swapped(send)
    near_mid = paired(near_out, 0)
    far_mid = paired(far_out, 1)

    def finish(near_mid, far_mid):
        return call(
            lambda *refs: last_kernel(width, *refs),
            [field, field],
            [patch],
            2 * conv_flops,
            movie_r, upstream_r, near_mid, far_mid, mid, grad, kernel_one, kernel_two,
        )

    scratch = [
        pltpu.VMEM((2 * ext, cells + 2 * width, TAPS * chans), BF16),
        pltpu.VMEM((chans, 2 * ext * cells), BF16),
    ]
    if dp == 2 and tm > 1 and tm & (tm - 1) == 0 and rows % 8 == 0:
        bits = tm.bit_length() - 1
        rest = [list(range(low, min(low + 2, bits))) for low in range(2, bits, 2)]
        orders = ([[0], [1]][:bits] + rest, [[1], [0]][2 - min(bits, 2) :] + rest)
        kept, sent = call(
            lambda *refs: relative_sums_kernel(width, distances(orders), *refs),
            [shape((tm // 2, rows, chans), F32), shape((tm // 2, rows, chans), BF16)],
            [pltpu.VMEM((krows, chans), F32)] + scratch,
            2 * conv_flops,
            keep, other,
        )
        sent, near_mid = lax.optimization_barrier((sent, near_mid))
        sends = [sent]
        for stage in range(len(orders[0])):
            steps = [distances([groups[stage : stage + 1]])[0] for groups in orders]
            gots = [
                exchanged(sends[q - 1], (steps[0][q], steps[1][q])) for q in reversed(range(1, len(steps[0])))
            ]
            if stage == 0:
                *gots, far_mid = lax.optimization_barrier((*gots, far_mid))
            if stage + 1 == len(orders[0]):
                output, movie_grad = finish(near_mid, far_mid)
                *gots, output, movie_grad = lax.optimization_barrier((*gots, output, movie_grad))
            for got in gots:
                kept = kept + got.astype(F32)
            if stage + 1 < len(orders[0]):
                parts = 1 << len(orders[0][stage + 1])
                size = kept.shape[0] // parts
                sends = [kept[q * size : (q + 1) * size].astype(BF16) for q in range(1, parts)]
                kept = kept[:size]
        mine = kept[0]
    else:
        (sums,) = call(
            lambda *refs: plain_sums_kernel(width, *refs),
            [shape((krows, chans), F32)],
            scratch,
            2 * conv_flops,
            keep, other,
        )
        output, movie_grad = finish(near_mid, far_mid)
        mine = lax.psum_scatter(sums, "tm", scatter_dimension=0, tiled=True)
        if dp > 2:
            groups = [[d for d in range(dp) if d % 2 == parity] for parity in range(2)]
            mine = lax.psum(mine, "dp", axis_index_groups=groups)
    theirs = swapped(mine)
    is_even = lax.axis_index("dp") % 2 == 0
    grad_one = jnp.where(is_even, mine, theirs)
    grad_two = jnp.where(is_even, theirs, mine)
    return (output.reshape(movie.shape), movie_grad.reshape(movie.shape), grad_one, grad_two)


def solution(mesh):
    in_specs = (P("dp", "tm", None, None, None), P(), P(), P("dp", "tm", None, None, None))
    out_specs = (
        P("dp", "tm", None, None, None),
        P("dp", "tm", None, None, None),
        P("tm", None),
        P("tm", None),
    )
    return jax.shard_map(body, mesh=mesh, in_specs=in_specs, out_specs=out_specs, check_vma=False)
```

```python
import jax
import jax.numpy as jnp
from jax import lax
from jax.experimental import pallas as pl
from jax.experimental.pallas import tpu as pltpu
from jax.sharding import PartitionSpec as P

BF16 = jnp.bfloat16
F32 = jnp.float32
TAPS = 3


def silu_grad(value):
    sig = jax.nn.sigmoid(value)
    return sig * (1.0 + value * (1.0 - sig))


def fill(patches, first, field, width, mirrored):
    frames, cells, chans = field.shape
    rows = frames * cells
    flat = field.astype(F32).reshape(rows, chans)
    column = lax.broadcasted_iota(jnp.int32, (rows, chans), 0) % width
    before = jnp.where(column == 0, 0.0, pltpu.roll(flat, 1, 0))
    after = jnp.where(column == width - 1, 0.0, pltpu.roll(flat, rows - 1, 0))
    blocks = (after, flat, before) if mirrored else (before, flat, after)
    for k, block in enumerate(blocks):
        patches[pl.ds(first, frames), width : width + cells, k * chans : (k + 1) * chans] = (
            block.astype(BF16).reshape(frames, cells, chans)
        )
    edge = jnp.zeros((frames, width, TAPS * chans), BF16)
    patches[pl.ds(first, frames), :width, :] = edge
    patches[pl.ds(first, frames), width + cells :, :] = edge


def conv_forward(patches, kernel, frames, cells, width):
    chans = kernel.shape[1]
    left = jnp.concatenate(
        [
            patches[kt : kt + frames, ki * width : ki * width + cells, :].reshape(frames * cells, TAPS * chans)
            for kt in range(TAPS)
            for ki in range(TAPS)
        ],
        axis=1,
    )
    return jnp.dot(left, kernel[...], preferred_element_type=F32)


def conv_backward(patches, kernel, frames, cells, width):
    chans = kernel.shape[1]
    left = jnp.concatenate(
        [
            patches[
                TAPS - 1 - kt : TAPS - 1 - kt + frames,
                (TAPS - 1 - ki) * width : (TAPS - 1 - ki) * width + cells,
                :,
            ].reshape(frames * cells, TAPS * chans)
            for kt in range(TAPS)
            for ki in range(TAPS)
        ],
        axis=1,
    )
    right = jnp.concatenate([kernel[tap * chans : (tap + 1) * chans, :] for tap in range(TAPS**3)], axis=1)
    return lax.dot_general(left, right, (((1,), (1,)), ((), ())), preferred_element_type=F32)


def taps_forward(patches, kernel, kt, first, count, cells, width):
    chans = kernel.shape[1]
    left = jnp.concatenate(
        [
            patches[first : first + count, ki * width : ki * width + cells, :].reshape(count * cells, TAPS * chans)
            for ki in range(TAPS)
        ],
        axis=1,
    )
    rows = TAPS * TAPS * chans
    return jnp.dot(left, kernel[kt * rows : (kt + 1) * rows, :], preferred_element_type=F32)


def taps_backward(patches, kernel, kt, first, count, cells, width):
    chans = kernel.shape[1]
    left = jnp.concatenate(
        [
            patches[
                first : first + count, (TAPS - 1 - ki) * width : (TAPS - 1 - ki) * width + cells, :
            ].reshape(count * cells, TAPS * chans)
            for ki in range(TAPS)
        ],
        axis=1,
    )
    taps = range(kt * TAPS * TAPS, (kt + 1) * TAPS * TAPS)
    right = jnp.concatenate([kernel[tap * chans : (tap + 1) * chans, :] for tap in taps], axis=1)
    return lax.dot_general(left, right, (((1,), (1,)), ((), ())), preferred_element_type=F32)


def edges_kernel(movie, upstream, near, far, sems):
    frames = movie.shape[0]
    halo = near.shape[0]
    even = lax.axis_index("tm") % 2 == 0

    def run(forward, backward):
        copies = [
            pltpu.make_async_copy(movie.at[pl.ds(frames - halo, halo)], forward, sems.at[0]),
            pltpu.make_async_copy(upstream.at[pl.ds(0, halo)], backward, sems.at[1]),
        ]
        for copy in copies:
            copy.start()
        for copy in copies:
            copy.wait()

    @pl.when(even)
    def _():
        run(near, far)

    @pl.when(jnp.logical_not(even))
    def _():
        run(far, near)


def sorted_edges(near, far):
    even = lax.axis_index("tm") % 2 == 0
    return jnp.where(even, far[...], near[...]), jnp.where(even, near[...], far[...])


def inner_kernel(
    width, movie, upstream, one, two, act_in, pre_part, grad_part, act_patches, up_patches
):
    frames, cells, chans = movie.shape
    act_in[...] = jax.nn.silu(movie[...].astype(F32)).astype(BF16)
    fill(act_patches, 0, act_in[...], width, False)
    fill(up_patches, 0, upstream[...], width, True)
    pre_part[...] = taps_forward(act_patches, one, TAPS - 1, 0, frames, cells, width)
    for lag in range(1, TAPS):
        part = taps_forward(act_patches, one, TAPS - 1 - lag, 0, frames - lag, cells, width)
        pre_part[lag * cells :, :] += part
    grad_part[...] = taps_backward(up_patches, two, TAPS - 1, 0, frames, cells, width)
    for lag in range(1, TAPS):
        part = taps_backward(up_patches, two, TAPS - 1 - lag, lag, frames - lag, cells, width)
        grad_part[: (frames - lag) * cells, :] += part


def outer_kernel(
    width, far, near, act_in, upstream, pre_part, grad_part, one, two, keep, send, mid, grad, near_out, far_out, patches
):
    frames, cells, chans = act_in.shape
    halo = TAPS - 1
    before, after = sorted_edges(near, far)
    act_before = jax.nn.silu(before.astype(F32)).astype(BF16)
    fill(patches, 0, act_before, width, False)
    pres = [pre_part[t * cells : (t + 1) * cells, :] for t in range(frames)]
    for kt in range(halo):
        part = taps_forward(patches, one, kt, kt, halo - kt, cells, width)
        for t in range(halo - kt):
            pres[t] = pres[t] + part[t * cells : (t + 1) * cells]
    pre = jnp.concatenate(pres, axis=0)
    act_mid = jax.nn.silu(pre).astype(BF16).reshape(frames, cells, chans)
    mid[...] = act_mid
    fill(patches, 0, after, width, True)
    grads = [grad_part[t * cells : (t + 1) * cells, :] for t in range(frames)]
    for kt in range(halo):
        part = taps_backward(patches, two, kt, 0, halo - kt, cells, width)
        for n in range(halo - kt):
            t = frames - (halo - kt) + n
            grads[t] = grads[t] + part[n * cells : (n + 1) * cells]
    mid_grad = jnp.concatenate(grads, axis=0)
    pre_grad = (mid_grad * silu_grad(pre)).astype(BF16).reshape(frames, cells, chans)
    grad[...] = pre_grad
    even = lax.axis_index("tm") % 2 == 0
    mid_tail, grad_head = act_mid[frames - halo :], pre_grad[:halo]
    near_out[...] = jnp.where(even, mid_tail, grad_head)
    far_out[...] = jnp.where(even, grad_head, mid_tail)

    def store(for_one, for_two):
        for_one[:frames] = grad[...]
        for_one[frames : frames + halo] = act_before
        for_one[frames + halo :] = act_in[...]
        for_two[:frames] = mid[...]
        for_two[frames : 2 * frames] = upstream[...]
        for_two[2 * frames :] = after

    is_even = lax.axis_index("dp") % 2 == 0

    @pl.when(is_even)
    def _():
        store(keep, send)

    @pl.when(jnp.logical_not(is_even))
    def _():
        store(send, keep)


def kernel_sums(width, own, other, acc, patches, turned):
    chans = own.shape[2]
    cells = own.shape[1]
    halo = TAPS - 1
    frames = (own.shape[0] - halo) // 2
    ext = frames + halo
    odd = lax.axis_index("dp") % 2
    for clip, source in enumerate((own, other)):
        fill(patches, clip * ext, source[pl.ds(odd * frames, ext)], width, True)
        for n in range(ext):
            block = source[(1 - odd) * frames + n]
            place = (clip * ext + n) * cells
            turned[:, place : place + cells] = block.astype(F32).T.astype(BF16)
    for kt in range(TAPS):
        l_start = (1 - odd) * kt
        r_start = odd * (halo - kt)
        left = jnp.concatenate(
            [
                turned[:, pl.ds(pl.multiple_of((clip * ext + l_start) * cells, cells), frames * cells)]
                for clip in range(2)
            ],
            axis=1,
        )
        for ki in range(TAPS):
            low = (halo - ki) * width
            right = jnp.concatenate(
                [
                    patches[pl.ds(clip * ext + r_start, frames), low : low + cells, :].reshape(
                        frames * cells, TAPS * chans
                    )
                    for clip in range(2)
                ],
                axis=0,
            )
            sums = jnp.dot(left, right, preferred_element_type=F32)
            for kj in range(TAPS):
                row = ((kt * TAPS + ki) * TAPS + kj) * chans
                acc[row : row + chans, :] = sums[:, kj * chans : (kj + 1) * chans]


def plain_sums_kernel(width, own, other, acc, patches, turned):
    kernel_sums(width, own, other, acc, patches, turned)


def relative_sums_kernel(width, distance, own, other, stay, pass_on, send_stay, send_on, acc, patches, turned):
    kernel_sums(width, own, other, acc, patches, turned)
    size, rows, _ = stay.shape
    odd = lax.axis_index("dp") % 2
    me = lax.axis_index("tm")
    for n, quarter in enumerate((stay, pass_on, send_stay, send_on)):
        for r in range(size):
            far = jnp.where(odd == 1, distance[1][n * size + r], distance[0][n * size + r])
            block = jnp.bitwise_xor(me, far)
            part = acc[pl.ds(pl.multiple_of(block * rows, 8), rows), :]
            quarter[r] = part.astype(quarter.dtype)


def last_kernel(width, movie, upstream, near, far, mid, grad, one, two, output, movie_grad, patches):
    frames, cells, chans = movie.shape
    mid_before, grad_after = sorted_edges(near, far)
    fill(patches, 0, jnp.concatenate([mid_before, mid[...]], axis=0), width, False)
    out = conv_forward(patches, two, frames, cells, width).reshape(frames, cells, chans)
    movie_f = movie[...].astype(F32)
    output[...] = (movie_f + out).astype(BF16)
    fill(patches, 0, jnp.concatenate([grad[...], grad_after], axis=0), width, True)
    in_grad = conv_backward(patches, one, frames, cells, width).reshape(frames, cells, chans)
    movie_grad[...] = (upstream[...].astype(F32) + in_grad * silu_grad(movie_f)).astype(BF16)


def call(body, outs, scratch, flops, *args, unplaced=(), limit=24):
    vmem = pl.BlockSpec(memory_space=pltpu.VMEM)
    anywhere = pl.BlockSpec(memory_space=pltpu.MemorySpace.HBM)
    size = sum(a.size * a.dtype.itemsize for a in args) + sum(o.size * o.dtype.itemsize for o in outs)
    return pl.pallas_call(
        body,
        out_shape=outs,
        in_specs=[anywhere if i in unplaced else vmem for i in range(len(args))],
        out_specs=[vmem] * len(outs),
        scratch_shapes=scratch,
        compiler_params=pltpu.CompilerParams(vmem_limit_bytes=int(limit * 2**20)),
        cost_estimate=pl.CostEstimate(flops=flops, bytes_accessed=size, transcendentals=0),
    )(*args)


def paired(block, first):
    pairs = [(i, i + 1) for i in range(first, lax.axis_size("tm") - 1, 2)]
    return lax.ppermute(block, "tm", pairs + [(j, i) for i, j in pairs])


def swapped(block):
    return lax.ppermute(block, "dp", [(i, i ^ 1) for i in range(lax.axis_size("dp"))])


def exchanged(send, steps):
    tm, dp = lax.axis_size("tm"), lax.axis_size("dp")
    route = [(t * dp + d, (t ^ steps[d % 2]) * dp + d) for t in range(tm) for d in range(dp)]
    return lax.ppermute(send, ("tm", "dp"), route)


def body(movie, kernel_one, kernel_two, upstream):
    clips, frames, height, width, chans = movie.shape
    assert clips == 1
    tm, dp = lax.axis_size("tm"), lax.axis_size("dp")
    assert dp % 2 == 0
    cells = height * width
    halo = TAPS - 1
    ext = frames + halo
    krows = kernel_one.shape[0]
    rows = krows // tm
    shape = jax.ShapeDtypeStruct
    flat = (frames, cells, chans)
    movie_r = movie.reshape(flat)
    upstream_r = upstream.reshape(flat)
    conv_flops = 2 * frames * cells * krows * chans
    patch = pltpu.VMEM((ext, cells + 2 * width, TAPS * chans), BF16)

    bundle = shape((frames + ext, cells, chans), BF16)
    field = shape(flat, BF16)
    edge = shape((halo, cells, chans), BF16)
    part = shape((frames * cells, chans), F32)
    own_patch = shape((frames, cells + 2 * width, TAPS * chans), BF16)

    near, far = call(
        edges_kernel,
        [edge, edge],
        [pltpu.SemaphoreType.DMA((2,))],
        8000000000,
        movie_r, upstream_r,
        unplaced=(0, 1),
        limit=53.8,
    )
    far = paired(far, 1)
    near = paired(near, 0)
    act_in, pre_part, grad_part = call(
        lambda *refs: inner_kernel(width, *refs),
        [field, part, part],
        [pltpu.VMEM(own_patch.shape, BF16)] * 2,
        3 * conv_flops // 2,
        movie_r, upstream_r, kernel_one, kernel_two,
    )
    keep, send, mid, grad, near_out, far_out = call(
        lambda *refs: outer_kernel(width, *refs),
        [bundle, bundle, field, field, edge, edge],
        [pltpu.VMEM((halo, cells + 2 * width, TAPS * chans), BF16)],
        conv_flops // 2,
        far, near, act_in, upstream_r, pre_part, grad_part, kernel_one, kernel_two,
    )
    other = swapped(send)
    near_mid = paired(near_out, 0)
    far_mid = paired(far_out, 1)

    def finish(near_mid, far_mid):
        return call(
            lambda *refs: last_kernel(width, *refs),
            [field, field],
            [patch],
            2 * conv_flops,
            movie_r, upstream_r, near_mid, far_mid, mid, grad, kernel_one, kernel_two,
        )

    scratch = [
        pltpu.VMEM((2 * ext, cells + 2 * width, TAPS * chans), BF16),
        pltpu.VMEM((chans, 2 * ext * cells), BF16),
    ]
    if dp == 2 and tm >= 4 and tm & (tm - 1) == 0 and rows % 8 == 0:
        size = tm // 4
        orders = ((1, 2), (2, 1))
        distance = [
            [a * first + b * second + 4 * q for a in range(2) for b in range(2) for q in range(size)]
            for first, second in orders
        ]
        wide, narrow = shape((size, rows, chans), F32), shape((size, rows, chans), BF16)
        stay, pass_on, send_stay, send_on = call(
            lambda *refs: relative_sums_kernel(width, distance, *refs),
            [wide, wide, narrow, narrow],
            [pltpu.VMEM((krows, chans), F32)] + scratch,
            2 * conv_flops,
            keep, other,
        )
        send_on, near_mid = lax.optimization_barrier((send_on, near_mid))
        got_on = exchanged(send_on, (orders[0][0], orders[1][0]))
        got_stay = exchanged(send_stay, (orders[0][0], orders[1][0]))
        got = exchanged((pass_on + got_on.astype(F32)).astype(BF16), (orders[0][1], orders[1][1]))
        kept = stay + got_stay.astype(F32) + got.astype(F32)
        gots = [exchanged(kept[q].astype(BF16), (4 * q, 4 * q)) for q in reversed(range(1, size))]
        output, movie_grad = finish(near_mid, far_mid)
        *gots, output, movie_grad = lax.optimization_barrier((*gots, output, movie_grad))
        mine = kept[0]
        for got in gots:
            mine = mine + got.astype(F32)
    else:
        (sums,) = call(
            lambda *refs: plain_sums_kernel(width, *refs),
            [shape((krows, chans), F32)],
            scratch,
            2 * conv_flops,
            keep, other,
        )
        output, movie_grad = finish(near_mid, far_mid)
        mine = lax.psum_scatter(sums, "tm", scatter_dimension=0, tiled=True)
        if dp > 2:
            groups = [[d for d in range(dp) if d % 2 == parity] for parity in range(2)]
            mine = lax.psum(mine, "dp", axis_index_groups=groups)
    theirs = swapped(mine)
    is_even = lax.axis_index("dp") % 2 == 0
    grad_one = jnp.where(is_even, mine, theirs)
    grad_two = jnp.where(is_even, theirs, mine)
    return (output.reshape(movie.shape), movie_grad.reshape(movie.shape), grad_one, grad_two)


def solution(mesh):
    in_specs = (P("dp", "tm", None, None, None), P(), P(), P("dp", "tm", None, None, None))
    out_specs = (
        P("dp", "tm", None, None, None),
        P("dp", "tm", None, None, None),
        P("tm", None),
        P("tm", None),
    )
    return jax.shard_map(body, mesh=mesh, in_specs=in_specs, out_specs=out_specs, check_vma=False)
```

```python
import jax
import jax.numpy as jnp
from jax import lax
from jax.experimental import pallas as pl
from jax.experimental.pallas import tpu as pltpu
from jax.sharding import PartitionSpec as P

BF16 = jnp.bfloat16
F32 = jnp.float32
TAPS = 3


def silu_grad(value):
    sig = jax.nn.sigmoid(value)
    return sig * (1.0 + value * (1.0 - sig))


def fill(patches, first, field, width, mirrored):
    frames, cells, chans = field.shape
    rows = frames * cells
    flat = field.astype(F32).reshape(rows, chans)
    column = lax.broadcasted_iota(jnp.int32, (rows, chans), 0) % width
    before = jnp.where(column == 0, 0.0, pltpu.roll(flat, 1, 0))
    after = jnp.where(column == width - 1, 0.0, pltpu.roll(flat, rows - 1, 0))
    blocks = (after, flat, before) if mirrored else (before, flat, after)
    for k, block in enumerate(blocks):
        patches[pl.ds(first, frames), width : width + cells, k * chans : (k + 1) * chans] = (
            block.astype(BF16).reshape(frames, cells, chans)
        )
    edge = jnp.zeros((frames, width, TAPS * chans), BF16)
    patches[pl.ds(first, frames), :width, :] = edge
    patches[pl.ds(first, frames), width + cells :, :] = edge


def taps_forward(patches, kernel, kt, first, count, cells, width):
    chans = kernel.shape[1]
    left = jnp.concatenate(
        [
            patches[first : first + count, ki * width : ki * width + cells, :].reshape(count * cells, TAPS * chans)
            for ki in range(TAPS)
        ],
        axis=1,
    )
    rows = TAPS * TAPS * chans
    return jnp.dot(left, kernel[kt * rows : (kt + 1) * rows, :], preferred_element_type=F32)


def taps_backward(patches, kernel, kt, first, count, cells, width):
    chans = kernel.shape[1]
    left = jnp.concatenate(
        [
            patches[
                first : first + count, (TAPS - 1 - ki) * width : (TAPS - 1 - ki) * width + cells, :
            ].reshape(count * cells, TAPS * chans)
            for ki in range(TAPS)
        ],
        axis=1,
    )
    taps = range(kt * TAPS * TAPS, (kt + 1) * TAPS * TAPS)
    right = jnp.concatenate([kernel[tap * chans : (tap + 1) * chans, :] for tap in taps], axis=1)
    return lax.dot_general(left, right, (((1,), (1,)), ((), ())), preferred_element_type=F32)


def edges_kernel(movie, upstream, near, far, sems):
    frames = movie.shape[0]
    halo = near.shape[0]
    even = lax.axis_index("tm") % 2 == 0

    def run(forward, backward):
        copies = [
            pltpu.make_async_copy(movie.at[pl.ds(frames - halo, halo)], forward, sems.at[0]),
            pltpu.make_async_copy(upstream.at[pl.ds(0, halo)], backward, sems.at[1]),
        ]
        for copy in copies:
            copy.start()
        for copy in copies:
            copy.wait()

    @pl.when(even)
    def _():
        run(near, far)

    @pl.when(jnp.logical_not(even))
    def _():
        run(far, near)


def sorted_edges(near, far):
    even = lax.axis_index("tm") % 2 == 0
    return jnp.where(even, far[...], near[...]), jnp.where(even, near[...], far[...])


def own_forward(patches, kernel, out, frames, cells, width):
    out[...] = taps_forward(patches, kernel, TAPS - 1, 0, frames, cells, width)
    for lag in range(1, TAPS):
        out[lag * cells :, :] += taps_forward(patches, kernel, TAPS - 1 - lag, 0, frames - lag, cells, width)


def own_backward(patches, kernel, out, frames, cells, width):
    out[...] = taps_backward(patches, kernel, TAPS - 1, 0, frames, cells, width)
    for lag in range(1, TAPS):
        part = taps_backward(patches, kernel, TAPS - 1 - lag, lag, frames - lag, cells, width)
        out[: (frames - lag) * cells, :] += part


def with_before(width, part, patches, kernel, before):
    _, cells, chans = before.shape
    fill(patches, 0, before, width, False)
    sums = [part[row : row + cells, :] for row in range(0, part.shape[0], cells)]
    for kt in range(TAPS - 1):
        count = TAPS - 1 - kt
        more = taps_forward(patches, kernel, kt, kt, count, cells, width)
        for n in range(count):
            sums[n] = sums[n] + more[n * cells : (n + 1) * cells]
    return jnp.concatenate(sums, axis=0)


def with_after(width, part, patches, kernel, after):
    _, cells, chans = after.shape
    fill(patches, 0, after, width, True)
    sums = [part[row : row + cells, :] for row in range(0, part.shape[0], cells)]
    for kt in range(TAPS - 1):
        count = TAPS - 1 - kt
        more = taps_backward(patches, kernel, kt, 0, count, cells, width)
        for n in range(count):
            sums[n - count] = sums[n - count] + more[n * cells : (n + 1) * cells]
    return jnp.concatenate(sums, axis=0)


def inner_kernel(width, movie, upstream, one, two, act_in, pre_part, grad_part, act_patches, up_patches):
    frames, cells, _ = movie.shape
    act_in[...] = jax.nn.silu(movie[...].astype(F32)).astype(BF16)
    fill(act_patches, 0, act_in[...], width, False)
    own_forward(act_patches, one, pre_part, frames, cells, width)
    fill(up_patches, 0, upstream[...], width, True)
    own_backward(up_patches, two, grad_part, frames, cells, width)


def outer_kernel(
    width, far, near, act_in, upstream, pre_part, grad_part, one, two, keep, send, mid, grad, near_out, far_out, patches
):
    frames, cells, chans = act_in.shape
    halo = TAPS - 1
    before, after = sorted_edges(near, far)
    act_before = jax.nn.silu(before.astype(F32)).astype(BF16)
    pre = with_before(width, pre_part, patches, one, act_before)
    act_mid = jax.nn.silu(pre).astype(BF16).reshape(frames, cells, chans)
    mid[...] = act_mid
    mid_grad = with_after(width, grad_part, patches, two, after)
    pre_grad = (mid_grad * silu_grad(pre)).astype(BF16).reshape(frames, cells, chans)
    grad[...] = pre_grad
    even = lax.axis_index("tm") % 2 == 0
    mid_tail, grad_head = act_mid[frames - halo :], pre_grad[:halo]
    near_out[...] = jnp.where(even, mid_tail, grad_head)
    far_out[...] = jnp.where(even, grad_head, mid_tail)

    def store(for_one, for_two):
        for_one[:frames] = grad[...]
        for_one[frames : frames + halo] = act_before
        for_one[frames + halo :] = act_in[...]
        for_two[:frames] = mid[...]
        for_two[frames : 2 * frames] = upstream[...]
        for_two[2 * frames :] = after

    is_even = lax.axis_index("dp") % 2 == 0

    @pl.when(is_even)
    def _():
        store(keep, send)

    @pl.when(jnp.logical_not(is_even))
    def _():
        store(send, keep)


def kernel_sums(width, own, other, acc, patches, turned):
    chans = own.shape[2]
    cells = own.shape[1]
    halo = TAPS - 1
    frames = (own.shape[0] - halo) // 2
    ext = frames + halo
    odd = lax.axis_index("dp") % 2
    for clip, source in enumerate((own, other)):
        fill(patches, clip * ext, source[pl.ds(odd * frames, ext)], width, True)
        for n in range(ext):
            block = source[(1 - odd) * frames + n]
            place = (clip * ext + n) * cells
            turned[:, place : place + cells] = block.T
    for kt in range(TAPS):
        l_start = (1 - odd) * kt
        r_start = odd * (halo - kt)
        left = jnp.concatenate(
            [
                turned[:, pl.ds(pl.multiple_of((clip * ext + l_start) * cells, cells), frames * cells)]
                for clip in range(2)
            ],
            axis=1,
        )
        for ki in range(TAPS):
            low = (halo - ki) * width
            right = jnp.concatenate(
                [
                    patches[pl.ds(clip * ext + r_start, frames), low : low + cells, :].reshape(
                        frames * cells, TAPS * chans
                    )
                    for clip in range(2)
                ],
                axis=0,
            )
            sums = jnp.dot(left, right, preferred_element_type=F32)
            for kj in range(TAPS):
                row = ((kt * TAPS + ki) * TAPS + kj) * chans
                acc[row : row + chans, :] = sums[:, kj * chans : (kj + 1) * chans]


def plain_sums_kernel(width, own, other, acc, patches, turned):
    kernel_sums(width, own, other, acc, patches, turned)


def relative_sums_kernel(width, distance, own, other, stay, pass_on, send_stay, send_on, acc, patches, turned):
    kernel_sums(width, own, other, acc, patches, turned)
    size, rows, _ = stay.shape
    odd = lax.axis_index("dp") % 2
    me = lax.axis_index("tm")
    for n, quarter in enumerate((stay, pass_on, send_stay, send_on)):
        for r in range(size):
            far = jnp.where(odd == 1, distance[1][n * size + r], distance[0][n * size + r])
            block = jnp.bitwise_xor(me, far)
            part = acc[pl.ds(pl.multiple_of(block * rows, 8), rows), :]
            quarter[r] = part.astype(quarter.dtype)


def middle_kernel(width, mid, grad, one, two, out_part, in_part, mid_patches, grad_patches):
    frames, cells, _ = mid.shape
    fill(mid_patches, 0, mid[...], width, False)
    own_forward(mid_patches, two, out_part, frames, cells, width)
    fill(grad_patches, 0, grad[...], width, True)
    own_backward(grad_patches, one, in_part, frames, cells, width)


def last_kernel(width, movie, upstream, near, far, out_part, in_part, one, two, output, movie_grad, patches):
    shape = movie.shape
    mid_before, grad_after = sorted_edges(near, far)
    movie_f = movie[...].astype(F32)
    out = with_before(width, out_part, patches, two, mid_before).reshape(shape)
    output[...] = (movie_f + out).astype(BF16)
    in_grad = with_after(width, in_part, patches, one, grad_after).reshape(shape)
    movie_grad[...] = (upstream[...].astype(F32) + in_grad * silu_grad(movie_f)).astype(BF16)


def call(body, outs, scratch, flops, *args, unplaced=(), limit=24):
    vmem = pl.BlockSpec(memory_space=pltpu.VMEM)
    anywhere = pl.BlockSpec(memory_space=pltpu.MemorySpace.HBM)
    size = sum(a.size * a.dtype.itemsize for a in args) + sum(o.size * o.dtype.itemsize for o in outs)
    return pl.pallas_call(
        body,
        out_shape=outs,
        in_specs=[anywhere if i in unplaced else vmem for i in range(len(args))],
        out_specs=[vmem] * len(outs),
        scratch_shapes=scratch,
        compiler_params=pltpu.CompilerParams(vmem_limit_bytes=int(limit * 2**20)),
        cost_estimate=pl.CostEstimate(flops=flops, bytes_accessed=size, transcendentals=0),
    )(*args)


def paired(block, first):
    pairs = [(i, i + 1) for i in range(first, lax.axis_size("tm") - 1, 2)]
    return lax.ppermute(block, "tm", pairs + [(j, i) for i, j in pairs])


def swapped(block):
    return lax.ppermute(block, "dp", [(i, i ^ 1) for i in range(lax.axis_size("dp"))])


def exchanged(send, steps):
    tm, dp = lax.axis_size("tm"), lax.axis_size("dp")
    route = [(t * dp + d, (t ^ steps[d % 2]) * dp + d) for t in range(tm) for d in range(dp)]
    return lax.ppermute(send, ("tm", "dp"), route)


def body(movie, kernel_one, kernel_two, upstream):
    clips, frames, height, width, chans = movie.shape
    assert clips == 1
    tm, dp = lax.axis_size("tm"), lax.axis_size("dp")
    assert dp % 2 == 0
    cells = height * width
    halo = TAPS - 1
    ext = frames + halo
    krows = kernel_one.shape[0]
    rows = krows // tm
    shape = jax.ShapeDtypeStruct
    flat = (frames, cells, chans)
    movie_r = movie.reshape(flat)
    upstream_r = upstream.reshape(flat)
    conv_flops = 2 * frames * cells * krows * chans

    bundle = shape((frames + ext, cells, chans), BF16)
    field = shape(flat, BF16)
    edge = shape((halo, cells, chans), BF16)
    part = shape((frames * cells, chans), F32)
    own_patch = shape((frames, cells + 2 * width, TAPS * chans), BF16)

    near, far = call(
        edges_kernel,
        [edge, edge],
        [pltpu.SemaphoreType.DMA((2,))],
        8000000000,
        movie_r, upstream_r,
        unplaced=(0, 1),
        limit=53.8,
    )
    far = paired(far, 1)
    near = paired(near, 0)
    act_in, pre_part, grad_part = call(
        lambda *refs: inner_kernel(width, *refs),
        [field, part, part],
        [pltpu.VMEM(own_patch.shape, BF16)] * 2,
        3 * conv_flops // 2,
        movie_r, upstream_r, kernel_one, kernel_two,
    )
    keep, send, mid, grad, near_out, far_out = call(
        lambda *refs: outer_kernel(width, *refs),
        [bundle, bundle, field, field, edge, edge],
        [pltpu.VMEM((halo, cells + 2 * width, TAPS * chans), BF16)],
        conv_flops // 2,
        far, near, act_in, upstream_r, pre_part, grad_part, kernel_one, kernel_two,
    )
    other = swapped(send)
    near_mid = paired(near_out, 0)
    far_mid = paired(far_out, 1)

    edge_patch = pltpu.VMEM((halo, cells + 2 * width, TAPS * chans), BF16)

    def middle(mid, grad):
        return call(
            lambda *refs: middle_kernel(width, *refs),
            [part, part],
            [pltpu.VMEM(own_patch.shape, BF16)] * 2,
            3 * conv_flops // 2,
            mid, grad, kernel_one, kernel_two,
        )

    def finish(near_mid, far_mid, out_part, in_part):
        return call(
            lambda *refs: last_kernel(width, *refs),
            [field, field],
            [edge_patch],
            conv_flops // 2,
            movie_r, upstream_r, near_mid, far_mid, out_part, in_part, kernel_one, kernel_two,
        )

    scratch = [
        pltpu.VMEM((2 * ext, cells + 2 * width, TAPS * chans), BF16),
        pltpu.VMEM((chans, 2 * ext * cells), BF16),
    ]
    if dp == 2 and tm >= 4 and tm & (tm - 1) == 0 and rows % 8 == 0:
        size = tm // 4
        orders = ((1, 2), (2, 1))
        distance = [
            [a * first + b * second + 4 * q for a in range(2) for b in range(2) for q in range(size)]
            for first, second in orders
        ]
        wide, narrow = shape((size, rows, chans), F32), shape((size, rows, chans), BF16)
        stay, pass_on, send_stay, send_on = call(
            lambda *refs: relative_sums_kernel(width, distance, *refs),
            [wide, wide, narrow, narrow],
            [pltpu.VMEM((krows, chans), F32)] + scratch,
            2 * conv_flops,
            keep, other,
        )
        send_on, near_mid, mid, grad = lax.optimization_barrier((send_on, near_mid, mid, grad))
        parts = middle(mid, grad)
        got_on = exchanged(send_on, (orders[0][0], orders[1][0]))
        got_stay = exchanged(send_stay, (orders[0][0], orders[1][0]))
        got_on, *parts = lax.optimization_barrier((got_on, *parts))
        got = exchanged((pass_on + got_on.astype(F32)).astype(BF16), (orders[0][1], orders[1][1]))
        kept = stay + got_stay.astype(F32) + got.astype(F32)
        gots = [exchanged(kept[q].astype(BF16), (4 * q, 4 * q)) for q in (2, 3, 1)]
        output, movie_grad = finish(near_mid, far_mid, *parts)
        *gots, output, movie_grad = lax.optimization_barrier((*gots, output, movie_grad))
        mine = kept[0]
        for got in gots:
            mine = mine + got.astype(F32)
    else:
        (sums,) = call(
            lambda *refs: plain_sums_kernel(width, *refs),
            [shape((krows, chans), F32)],
            scratch,
            2 * conv_flops,
            keep, other,
        )
        output, movie_grad = finish(near_mid, far_mid, *middle(mid, grad))
        mine = lax.psum_scatter(sums, "tm", scatter_dimension=0, tiled=True)
        if dp > 2:
            groups = [[d for d in range(dp) if d % 2 == parity] for parity in range(2)]
            mine = lax.psum(mine, "dp", axis_index_groups=groups)
    theirs = swapped(mine)
    is_even = lax.axis_index("dp") % 2 == 0
    grad_one = jnp.where(is_even, mine, theirs)
    grad_two = jnp.where(is_even, theirs, mine)
    return (output.reshape(movie.shape), movie_grad.reshape(movie.shape), grad_one, grad_two)


def solution(mesh):
    in_specs = (P("dp", "tm", None, None, None), P(), P(), P("dp", "tm", None, None, None))
    out_specs = (
        P("dp", "tm", None, None, None),
        P("dp", "tm", None, None, None),
        P("tm", None),
        P("tm", None),
    )
    return jax.shard_map(body, mesh=mesh, in_specs=in_specs, out_specs=out_specs, check_vma=False)
```

```python
import jax
import jax.numpy as jnp
from jax import lax
from jax.experimental import pallas as pl
from jax.experimental.pallas import tpu as pltpu
from jax.sharding import PartitionSpec as P

BF16 = jnp.bfloat16
F32 = jnp.float32
TAPS = 3


def silu_grad(value):
    sig = jax.nn.sigmoid(value)
    return sig * (1.0 + value * (1.0 - sig))


def fill(patches, first, field, width, mirrored):
    frames, cells, chans = field.shape
    rows = frames * cells
    flat = field.astype(F32).reshape(rows, chans)
    column = lax.broadcasted_iota(jnp.int32, (rows, chans), 0) % width
    before = jnp.where(column == 0, 0.0, pltpu.roll(flat, 1, 0))
    after = jnp.where(column == width - 1, 0.0, pltpu.roll(flat, rows - 1, 0))
    blocks = (after, flat, before) if mirrored else (before, flat, after)
    for k, block in enumerate(blocks):
        patches[pl.ds(first, frames), width : width + cells, k * chans : (k + 1) * chans] = (
            block.astype(BF16).reshape(frames, cells, chans)
        )
    edge = jnp.zeros((frames, width, TAPS * chans), BF16)
    patches[pl.ds(first, frames), :width, :] = edge
    patches[pl.ds(first, frames), width + cells :, :] = edge


def taps_forward(patches, kernel, kt, first, count, cells, width):
    chans = kernel.shape[1]
    left = jnp.concatenate(
        [
            patches[first : first + count, ki * width : ki * width + cells, :].reshape(count * cells, TAPS * chans)
            for ki in range(TAPS)
        ],
        axis=1,
    )
    rows = TAPS * TAPS * chans
    return jnp.dot(left, kernel[kt * rows : (kt + 1) * rows, :], preferred_element_type=F32)


def taps_backward(patches, kernel, kt, first, count, cells, width):
    chans = kernel.shape[1]
    left = jnp.concatenate(
        [
            patches[
                first : first + count, (TAPS - 1 - ki) * width : (TAPS - 1 - ki) * width + cells, :
            ].reshape(count * cells, TAPS * chans)
            for ki in range(TAPS)
        ],
        axis=1,
    )
    taps = range(kt * TAPS * TAPS, (kt + 1) * TAPS * TAPS)
    right = jnp.concatenate([kernel[tap * chans : (tap + 1) * chans, :] for tap in taps], axis=1)
    return lax.dot_general(left, right, (((1,), (1,)), ((), ())), preferred_element_type=F32)


def edges_kernel(movie, upstream, near, far, sems):
    frames = movie.shape[0]
    halo = near.shape[0]
    even = lax.axis_index("tm") % 2 == 0

    def run(forward, backward):
        copies = [
            pltpu.make_async_copy(movie.at[pl.ds(frames - halo, halo)], forward, sems.at[0]),
            pltpu.make_async_copy(upstream.at[pl.ds(0, halo)], backward, sems.at[1]),
        ]
        for copy in copies:
            copy.start()
        for copy in copies:
            copy.wait()

    @pl.when(even)
    def _():
        run(near, far)

    @pl.when(jnp.logical_not(even))
    def _():
        run(far, near)


def sorted_edges(near, far):
    even = lax.axis_index("tm") % 2 == 0
    return jnp.where(even, far[...], near[...]), jnp.where(even, near[...], far[...])


def own_forward(patches, kernel, out, frames, cells, width):
    out[...] = taps_forward(patches, kernel, TAPS - 1, 0, frames, cells, width)
    for lag in range(1, TAPS):
        out[lag * cells :, :] += taps_forward(patches, kernel, TAPS - 1 - lag, 0, frames - lag, cells, width)


def own_backward(patches, kernel, out, frames, cells, width):
    out[...] = taps_backward(patches, kernel, TAPS - 1, 0, frames, cells, width)
    for lag in range(1, TAPS):
        part = taps_backward(patches, kernel, TAPS - 1 - lag, lag, frames - lag, cells, width)
        out[: (frames - lag) * cells, :] += part


def with_before(width, part, patches, kernel, before):
    _, cells, chans = before.shape
    fill(patches, 0, before, width, False)
    sums = [part[row : row + cells, :] for row in range(0, part.shape[0], cells)]
    for kt in range(TAPS - 1):
        count = TAPS - 1 - kt
        more = taps_forward(patches, kernel, kt, kt, count, cells, width)
        for n in range(count):
            sums[n] = sums[n] + more[n * cells : (n + 1) * cells]
    return jnp.concatenate(sums, axis=0)


def with_after(width, part, patches, kernel, after):
    _, cells, chans = after.shape
    fill(patches, 0, after, width, True)
    sums = [part[row : row + cells, :] for row in range(0, part.shape[0], cells)]
    for kt in range(TAPS - 1):
        count = TAPS - 1 - kt
        more = taps_backward(patches, kernel, kt, 0, count, cells, width)
        for n in range(count):
            sums[n - count] = sums[n - count] + more[n * cells : (n + 1) * cells]
    return jnp.concatenate(sums, axis=0)


def inner_kernel(width, movie, upstream, one, two, act_in, pre_part, grad_part, act_patches, up_patches):
    frames, cells, _ = movie.shape
    act_in[...] = jax.nn.silu(movie[...].astype(F32)).astype(BF16)
    fill(act_patches, 0, act_in[...], width, False)
    own_forward(act_patches, one, pre_part, frames, cells, width)
    fill(up_patches, 0, upstream[...], width, True)
    own_backward(up_patches, two, grad_part, frames, cells, width)


def outer_kernel(
    width, far, near, act_in, upstream, pre_part, grad_part, one, two, keep, send, mid, grad, near_out, far_out, patches
):
    frames, cells, chans = act_in.shape
    halo = TAPS - 1
    before, after = sorted_edges(near, far)
    act_before = jax.nn.silu(before.astype(F32)).astype(BF16)
    pre = with_before(width, pre_part, patches, one, act_before)
    act_mid = jax.nn.silu(pre).astype(BF16).reshape(frames, cells, chans)
    mid[...] = act_mid
    mid_grad = with_after(width, grad_part, patches, two, after)
    pre_grad = (mid_grad * silu_grad(pre)).astype(BF16).reshape(frames, cells, chans)
    grad[...] = pre_grad
    even = lax.axis_index("tm") % 2 == 0
    mid_tail, grad_head = act_mid[frames - halo :], pre_grad[:halo]
    near_out[...] = jnp.where(even, mid_tail, grad_head)
    far_out[...] = jnp.where(even, grad_head, mid_tail)

    def store(for_one, for_two):
        for_one[:frames] = grad[...]
        for_one[frames : frames + halo] = act_before
        for_one[frames + halo :] = act_in[...]
        for_two[:frames] = mid[...]
        for_two[frames : 2 * frames] = upstream[...]
        for_two[2 * frames :] = after

    is_even = lax.axis_index("dp") % 2 == 0

    @pl.when(is_even)
    def _():
        store(keep, send)

    @pl.when(jnp.logical_not(is_even))
    def _():
        store(send, keep)


def kernel_sums(width, own, other, acc, patches, turned):
    chans = own.shape[2]
    cells = own.shape[1]
    halo = TAPS - 1
    frames = (own.shape[0] - halo) // 2
    ext = frames + halo
    odd = lax.axis_index("dp") % 2
    for clip, source in enumerate((own, other)):
        fill(patches, clip * ext, source[pl.ds(odd * frames, ext)], width, True)
        for n in range(ext):
            block = source[(1 - odd) * frames + n]
            place = (clip * ext + n) * cells
            turned[:, place : place + cells] = block.T
    for kt in range(TAPS):
        l_start = (1 - odd) * kt
        r_start = odd * (halo - kt)
        left = jnp.concatenate(
            [
                turned[:, pl.ds(pl.multiple_of((clip * ext + l_start) * cells, cells), frames * cells)]
                for clip in range(2)
            ],
            axis=1,
        )
        for ki in range(TAPS):
            low = (halo - ki) * width
            right = jnp.concatenate(
                [
                    patches[pl.ds(clip * ext + r_start, frames), low : low + cells, :].reshape(
                        frames * cells, TAPS * chans
                    )
                    for clip in range(2)
                ],
                axis=0,
            )
            sums = jnp.dot(left, right, preferred_element_type=F32)
            for kj in range(TAPS):
                row = ((kt * TAPS + ki) * TAPS + kj) * chans
                acc[row : row + chans, :] = sums[:, kj * chans : (kj + 1) * chans]


def plain_sums_kernel(width, own, other, acc, patches, turned):
    kernel_sums(width, own, other, acc, patches, turned)


def relative_sums_kernel(width, distance, own, other, stay, pass_on, send_stay, send_on, acc, patches, turned):
    kernel_sums(width, own, other, acc, patches, turned)
    size, rows, _ = stay.shape
    odd = lax.axis_index("dp") % 2
    me = lax.axis_index("tm")
    for n, quarter in enumerate((stay, pass_on, send_stay, send_on)):
        for r in range(size):
            far = jnp.where(odd == 1, distance[1][n * size + r], distance[0][n * size + r])
            block = jnp.bitwise_xor(me, far)
            part = acc[pl.ds(pl.multiple_of(block * rows, 8), rows), :]
            quarter[r] = part.astype(quarter.dtype)


def middle_kernel(width, mid, grad, one, two, out_part, in_part, mid_patches, grad_patches):
    frames, cells, _ = mid.shape
    fill(mid_patches, 0, mid[...], width, False)
    own_forward(mid_patches, two, out_part, frames, cells, width)
    fill(grad_patches, 0, grad[...], width, True)
    own_backward(grad_patches, one, in_part, frames, cells, width)


def last_kernel(width, movie, upstream, near, far, out_part, in_part, one, two, output, movie_grad, patches):
    shape = movie.shape
    mid_before, grad_after = sorted_edges(near, far)
    movie_f = movie[...].astype(F32)
    out = with_before(width, out_part, patches, two, mid_before).reshape(shape)
    output[...] = (movie_f + out).astype(BF16)
    in_grad = with_after(width, in_part, patches, one, grad_after).reshape(shape)
    movie_grad[...] = (upstream[...].astype(F32) + in_grad * silu_grad(movie_f)).astype(BF16)


def call(body, outs, scratch, flops, *args, unplaced=(), limit=24):
    vmem = pl.BlockSpec(memory_space=pltpu.VMEM)
    anywhere = pl.BlockSpec(memory_space=pltpu.MemorySpace.HBM)
    size = sum(a.size * a.dtype.itemsize for a in args) + sum(o.size * o.dtype.itemsize for o in outs)
    return pl.pallas_call(
        body,
        out_shape=outs,
        in_specs=[anywhere if i in unplaced else vmem for i in range(len(args))],
        out_specs=[vmem] * len(outs),
        scratch_shapes=scratch,
        compiler_params=pltpu.CompilerParams(vmem_limit_bytes=int(limit * 2**20)),
        cost_estimate=pl.CostEstimate(flops=flops, bytes_accessed=size, transcendentals=0),
    )(*args)


def paired(block, first):
    pairs = [(i, i + 1) for i in range(first, lax.axis_size("tm") - 1, 2)]
    return lax.ppermute(block, "tm", pairs + [(j, i) for i, j in pairs])


def swapped(block):
    return lax.ppermute(block, "dp", [(i, i ^ 1) for i in range(lax.axis_size("dp"))])


def exchanged(send, steps):
    tm, dp = lax.axis_size("tm"), lax.axis_size("dp")
    route = [(t * dp + d, (t ^ steps[d % 2]) * dp + d) for t in range(tm) for d in range(dp)]
    return lax.ppermute(send, ("tm", "dp"), route)


def body(movie, kernel_one, kernel_two, upstream):
    clips, frames, height, width, chans = movie.shape
    assert clips == 1
    tm, dp = lax.axis_size("tm"), lax.axis_size("dp")
    assert dp % 2 == 0
    cells = height * width
    halo = TAPS - 1
    ext = frames + halo
    krows = kernel_one.shape[0]
    rows = krows // tm
    shape = jax.ShapeDtypeStruct
    flat = (frames, cells, chans)
    movie_r = movie.reshape(flat)
    upstream_r = upstream.reshape(flat)
    conv_flops = 2 * frames * cells * krows * chans

    bundle = shape((frames + ext, cells, chans), BF16)
    field = shape(flat, BF16)
    edge = shape((halo, cells, chans), BF16)
    part = shape((frames * cells, chans), F32)
    own_patch = shape((frames, cells + 2 * width, TAPS * chans), BF16)

    near, far = call(
        edges_kernel,
        [edge, edge],
        [pltpu.SemaphoreType.DMA((2,))],
        8000000000,
        movie_r, upstream_r,
        unplaced=(0, 1),
        limit=53.8,
    )
    far = paired(far, 1)
    near = paired(near, 0)
    act_in, pre_part, grad_part = call(
        lambda *refs: inner_kernel(width, *refs),
        [field, part, part],
        [pltpu.VMEM(own_patch.shape, BF16)] * 2,
        3 * conv_flops // 2,
        movie_r, upstream_r, kernel_one, kernel_two,
    )
    keep, send, mid, grad, near_out, far_out = call(
        lambda *refs: outer_kernel(width, *refs),
        [bundle, bundle, field, field, edge, edge],
        [pltpu.VMEM((halo, cells + 2 * width, TAPS * chans), BF16)],
        conv_flops // 2,
        far, near, act_in, upstream_r, pre_part, grad_part, kernel_one, kernel_two,
    )
    other = swapped(send)
    near_mid = paired(near_out, 0)
    far_mid = paired(far_out, 1)

    edge_patch = pltpu.VMEM((halo, cells + 2 * width, TAPS * chans), BF16)

    def middle(mid, grad):
        return call(
            lambda *refs: middle_kernel(width, *refs),
            [part, part],
            [pltpu.VMEM(own_patch.shape, BF16)] * 2,
            3 * conv_flops // 2,
            mid, grad, kernel_one, kernel_two,
        )

    def finish(near_mid, far_mid, out_part, in_part):
        return call(
            lambda *refs: last_kernel(width, *refs),
            [field, field],
            [edge_patch],
            conv_flops // 2,
            movie_r, upstream_r, near_mid, far_mid, out_part, in_part, kernel_one, kernel_two,
        )

    scratch = [
        pltpu.VMEM((2 * ext, cells + 2 * width, TAPS * chans), BF16),
        pltpu.VMEM((chans, 2 * ext * cells), BF16),
    ]
    if dp == 2 and tm >= 4 and tm & (tm - 1) == 0 and rows % 8 == 0:
        size = tm // 4
        orders = ((1, 2), (2, 1))
        distance = [
            [a * first + b * second + 4 * q for a in range(2) for b in range(2) for q in range(size)]
            for first, second in orders
        ]
        wide, narrow = shape((size, rows, chans), F32), shape((size, rows, chans), BF16)
        stay, pass_on, send_stay, send_on = call(
            lambda *refs: relative_sums_kernel(width, distance, *refs),
            [wide, wide, narrow, narrow],
            [pltpu.VMEM((krows, chans), F32)] + scratch,
            2 * conv_flops,
            keep, other,
        )
        send_on, mid, grad = lax.optimization_barrier((send_on, mid, grad))
        parts = middle(mid, grad)
        got_on = exchanged(send_on, (orders[0][0], orders[1][0]))
        got_stay = exchanged(send_stay, (orders[0][0], orders[1][0]))
        got_on, *parts = lax.optimization_barrier((got_on, *parts))
        got = exchanged((pass_on + got_on.astype(F32)).astype(BF16), (orders[0][1], orders[1][1]))
        kept = stay + got_stay.astype(F32) + got.astype(F32)
        gots = [exchanged(kept[q].astype(BF16), (4 * q, 4 * q)) for q in (2, 3, 1)]
        output, movie_grad = finish(near_mid, far_mid, *parts)
        *gots, output, movie_grad = lax.optimization_barrier((*gots, output, movie_grad))
        mine = kept[0]
        for got in gots:
            mine = mine + got.astype(F32)
    else:
        (sums,) = call(
            lambda *refs: plain_sums_kernel(width, *refs),
            [shape((krows, chans), F32)],
            scratch,
            2 * conv_flops,
            keep, other,
        )
        output, movie_grad = finish(near_mid, far_mid, *middle(mid, grad))
        mine = lax.psum_scatter(sums, "tm", scatter_dimension=0, tiled=True)
        if dp > 2:
            groups = [[d for d in range(dp) if d % 2 == parity] for parity in range(2)]
            mine = lax.psum(mine, "dp", axis_index_groups=groups)
    theirs = swapped(mine)
    is_even = lax.axis_index("dp") % 2 == 0
    grad_one = jnp.where(is_even, mine, theirs)
    grad_two = jnp.where(is_even, theirs, mine)
    return (output.reshape(movie.shape), movie_grad.reshape(movie.shape), grad_one, grad_two)


def solution(mesh):
    in_specs = (P("dp", "tm", None, None, None), P(), P(), P("dp", "tm", None, None, None))
    out_specs = (
        P("dp", "tm", None, None, None),
        P("dp", "tm", None, None, None),
        P("tm", None),
        P("tm", None),
    )
    return jax.shard_map(body, mesh=mesh, in_specs=in_specs, out_specs=out_specs, check_vma=False)
```

```python
import jax
import jax.numpy as jnp
from jax import lax
from jax.experimental import pallas as pl
from jax.experimental.pallas import tpu as pltpu
from jax.sharding import PartitionSpec as P

BF16 = jnp.bfloat16
F32 = jnp.float32
TAPS = 3


def silu_grad(value):
    sig = jax.nn.sigmoid(value)
    return sig * (1.0 + value * (1.0 - sig))


def fill(patches, first, field, width, mirrored):
    frames, cells, chans = field.shape
    rows = frames * cells
    flat = field.astype(F32).reshape(rows, chans)
    column = lax.broadcasted_iota(jnp.int32, (rows, chans), 0) % width
    before = jnp.where(column == 0, 0.0, pltpu.roll(flat, 1, 0))
    after = jnp.where(column == width - 1, 0.0, pltpu.roll(flat, rows - 1, 0))
    blocks = (after, flat, before) if mirrored else (before, flat, after)
    for k, block in enumerate(blocks):
        patches[pl.ds(first, frames), width : width + cells, k * chans : (k + 1) * chans] = (
            block.astype(BF16).reshape(frames, cells, chans)
        )
    edge = jnp.zeros((frames, width, TAPS * chans), BF16)
    patches[pl.ds(first, frames), :width, :] = edge
    patches[pl.ds(first, frames), width + cells :, :] = edge


def taps_forward(patches, kernel, kt, first, count, cells, width):
    chans = kernel.shape[1]
    left = jnp.concatenate(
        [
            patches[first : first + count, ki * width : ki * width + cells, :].reshape(count * cells, TAPS * chans)
            for ki in range(TAPS)
        ],
        axis=1,
    )
    rows = TAPS * TAPS * chans
    return jnp.dot(left, kernel[kt * rows : (kt + 1) * rows, :], preferred_element_type=F32)


def taps_backward(patches, kernel, kt, first, count, cells, width):
    chans = kernel.shape[1]
    left = jnp.concatenate(
        [
            patches[
                first : first + count, (TAPS - 1 - ki) * width : (TAPS - 1 - ki) * width + cells, :
            ].reshape(count * cells, TAPS * chans)
            for ki in range(TAPS)
        ],
        axis=1,
    )
    taps = range(kt * TAPS * TAPS, (kt + 1) * TAPS * TAPS)
    right = jnp.concatenate([kernel[tap * chans : (tap + 1) * chans, :] for tap in taps], axis=1)
    return lax.dot_general(left, right, (((1,), (1,)), ((), ())), preferred_element_type=F32)


def edges_kernel(movie, upstream, near, far, sems):
    frames = movie.shape[0]
    halo = near.shape[0]
    even = lax.axis_index("tm") % 2 == 0

    def run(forward, backward):
        copies = [
            pltpu.make_async_copy(movie.at[pl.ds(frames - halo, halo)], forward, sems.at[0]),
            pltpu.make_async_copy(upstream.at[pl.ds(0, halo)], backward, sems.at[1]),
        ]
        for copy in copies:
            copy.start()
        for copy in copies:
            copy.wait()

    @pl.when(even)
    def _():
        run(near, far)

    @pl.when(jnp.logical_not(even))
    def _():
        run(far, near)


def sorted_edges(near, far):
    even = lax.axis_index("tm") % 2 == 0
    return jnp.where(even, far[...], near[...]), jnp.where(even, near[...], far[...])


def own_forward(patches, kernel, out, frames, cells, width):
    out[...] = taps_forward(patches, kernel, TAPS - 1, 0, frames, cells, width)
    for lag in range(1, TAPS):
        out[lag * cells :, :] += taps_forward(patches, kernel, TAPS - 1 - lag, 0, frames - lag, cells, width)


def own_backward(patches, kernel, out, frames, cells, width):
    out[...] = taps_backward(patches, kernel, TAPS - 1, 0, frames, cells, width)
    for lag in range(1, TAPS):
        part = taps_backward(patches, kernel, TAPS - 1 - lag, lag, frames - lag, cells, width)
        out[: (frames - lag) * cells, :] += part


def with_before(width, part, patches, kernel, before):
    _, cells, chans = before.shape
    fill(patches, 0, before, width, False)
    sums = [part[row : row + cells, :] for row in range(0, part.shape[0], cells)]
    for kt in range(TAPS - 1):
        count = TAPS - 1 - kt
        more = taps_forward(patches, kernel, kt, kt, count, cells, width)
        for n in range(count):
            sums[n] = sums[n] + more[n * cells : (n + 1) * cells]
    return jnp.concatenate(sums, axis=0)


def with_after(width, part, patches, kernel, after):
    _, cells, chans = after.shape
    fill(patches, 0, after, width, True)
    sums = [part[row : row + cells, :] for row in range(0, part.shape[0], cells)]
    for kt in range(TAPS - 1):
        count = TAPS - 1 - kt
        more = taps_backward(patches, kernel, kt, 0, count, cells, width)
        for n in range(count):
            sums[n - count] = sums[n - count] + more[n * cells : (n + 1) * cells]
    return jnp.concatenate(sums, axis=0)


def inner_kernel(width, movie, upstream, one, two, act_in, pre_part, grad_part, act_patches, up_patches):
    frames, cells, _ = movie.shape
    act_in[...] = jax.nn.silu(movie[...].astype(F32)).astype(BF16)
    fill(act_patches, 0, act_in[...], width, False)
    own_forward(act_patches, one, pre_part, frames, cells, width)
    fill(up_patches, 0, upstream[...], width, True)
    own_backward(up_patches, two, grad_part, frames, cells, width)


def outer_kernel(
    width, far, near, act_in, upstream, pre_part, grad_part, one, two, keep, send, mid, grad, near_out, far_out, patches
):
    frames, cells, chans = act_in.shape
    halo = TAPS - 1
    before, after = sorted_edges(near, far)
    act_before = jax.nn.silu(before.astype(F32)).astype(BF16)
    pre = with_before(width, pre_part, patches, one, act_before)
    act_mid = jax.nn.silu(pre).astype(BF16).reshape(frames, cells, chans)
    mid[...] = act_mid
    mid_grad = with_after(width, grad_part, patches, two, after)
    pre_grad = (mid_grad * silu_grad(pre)).astype(BF16).reshape(frames, cells, chans)
    grad[...] = pre_grad
    even = lax.axis_index("tm") % 2 == 0
    mid_tail, grad_head = act_mid[frames - halo :], pre_grad[:halo]
    near_out[...] = jnp.where(even, mid_tail, grad_head)
    far_out[...] = jnp.where(even, grad_head, mid_tail)

    def store(for_one, for_two):
        for_one[:frames] = grad[...]
        for_one[frames : frames + halo] = act_before
        for_one[frames + halo :] = act_in[...]
        for_two[:frames] = mid[...]
        for_two[frames : 2 * frames] = upstream[...]
        for_two[2 * frames :] = after

    is_even = lax.axis_index("dp") % 2 == 0

    @pl.when(is_even)
    def _():
        store(keep, send)

    @pl.when(jnp.logical_not(is_even))
    def _():
        store(send, keep)


def kernel_sums(width, source, acc, patches, turned, before=None):
    ext_frames, cells, chans = source.shape
    halo = TAPS - 1
    frames = (ext_frames - halo) // 2
    odd = lax.axis_index("dp") % 2
    fill(patches, 0, source[pl.ds(odd * frames, frames + halo)], width, True)
    for n in range(frames + halo):
        turned[:, n * cells : (n + 1) * cells] = source[(1 - odd) * frames + n].T
    for kt in range(TAPS):
        l_start = (1 - odd) * kt
        r_start = odd * (halo - kt)
        left = turned[:, pl.ds(pl.multiple_of(l_start * cells, cells), frames * cells)]
        for ki in range(TAPS):
            low = (halo - ki) * width
            right = patches[pl.ds(r_start, frames), low : low + cells, :].reshape(frames * cells, TAPS * chans)
            sums = jnp.dot(left, right, preferred_element_type=F32)
            for kj in range(TAPS):
                row = ((kt * TAPS + ki) * TAPS + kj) * chans
                part = sums[:, kj * chans : (kj + 1) * chans]
                if before is not None:
                    part = part + before[row : row + chans, :]
                acc[row : row + chans, :] = part


def own_sums_kernel(width, own, acc, patches, turned):
    kernel_sums(width, own, acc, patches, turned)


def plain_sums_kernel(width, own_sums, other, acc, patches, turned):
    kernel_sums(width, other, acc, patches, turned, own_sums)


def relative_sums_kernel(width, distance, own_sums, other, stay, pass_on, send_stay, send_on, acc, patches, turned):
    kernel_sums(width, other, acc, patches, turned, own_sums)
    size, rows, _ = stay.shape
    odd = lax.axis_index("dp") % 2
    me = lax.axis_index("tm")
    for n, quarter in enumerate((stay, pass_on, send_stay, send_on)):
        for r in range(size):
            far = jnp.where(odd == 1, distance[1][n * size + r], distance[0][n * size + r])
            block = jnp.bitwise_xor(me, far)
            part = acc[pl.ds(pl.multiple_of(block * rows, 8), rows), :]
            quarter[r] = part.astype(quarter.dtype)


def middle_kernel(width, mid, grad, one, two, out_part, in_part, mid_patches, grad_patches):
    frames, cells, _ = mid.shape
    fill(mid_patches, 0, mid[...], width, False)
    own_forward(mid_patches, two, out_part, frames, cells, width)
    fill(grad_patches, 0, grad[...], width, True)
    own_backward(grad_patches, one, in_part, frames, cells, width)


def last_kernel(width, movie, upstream, near, far, out_part, in_part, one, two, output, movie_grad, patches):
    shape = movie.shape
    mid_before, grad_after = sorted_edges(near, far)
    movie_f = movie[...].astype(F32)
    out = with_before(width, out_part, patches, two, mid_before).reshape(shape)
    output[...] = (movie_f + out).astype(BF16)
    in_grad = with_after(width, in_part, patches, one, grad_after).reshape(shape)
    movie_grad[...] = (upstream[...].astype(F32) + in_grad * silu_grad(movie_f)).astype(BF16)


def call(body, outs, scratch, flops, *args, unplaced=(), limit=24):
    vmem = pl.BlockSpec(memory_space=pltpu.VMEM)
    anywhere = pl.BlockSpec(memory_space=pltpu.MemorySpace.HBM)
    size = sum(a.size * a.dtype.itemsize for a in args) + sum(o.size * o.dtype.itemsize for o in outs)
    return pl.pallas_call(
        body,
        out_shape=outs,
        in_specs=[anywhere if i in unplaced else vmem for i in range(len(args))],
        out_specs=[vmem] * len(outs),
        scratch_shapes=scratch,
        compiler_params=pltpu.CompilerParams(vmem_limit_bytes=int(limit * 2**20)),
        cost_estimate=pl.CostEstimate(flops=flops, bytes_accessed=size, transcendentals=0),
    )(*args)


def paired(block, first):
    pairs = [(i, i + 1) for i in range(first, lax.axis_size("tm") - 1, 2)]
    return lax.ppermute(block, "tm", pairs + [(j, i) for i, j in pairs])


def swapped(block):
    return lax.ppermute(block, "dp", [(i, i ^ 1) for i in range(lax.axis_size("dp"))])


def exchanged(send, steps):
    tm, dp = lax.axis_size("tm"), lax.axis_size("dp")
    route = [(t * dp + d, (t ^ steps[d % 2]) * dp + d) for t in range(tm) for d in range(dp)]
    return lax.ppermute(send, ("tm", "dp"), route)


def body(movie, kernel_one, kernel_two, upstream):
    clips, frames, height, width, chans = movie.shape
    assert clips == 1
    tm, dp = lax.axis_size("tm"), lax.axis_size("dp")
    assert dp % 2 == 0
    cells = height * width
    halo = TAPS - 1
    ext = frames + halo
    krows = kernel_one.shape[0]
    rows = krows // tm
    shape = jax.ShapeDtypeStruct
    flat = (frames, cells, chans)
    movie_r = movie.reshape(flat)
    upstream_r = upstream.reshape(flat)
    conv_flops = 2 * frames * cells * krows * chans

    bundle = shape((frames + ext, cells, chans), BF16)
    field = shape(flat, BF16)
    edge = shape((halo, cells, chans), BF16)
    part = shape((frames * cells, chans), F32)
    own_patch = shape((frames, cells + 2 * width, TAPS * chans), BF16)

    near, far = call(
        edges_kernel,
        [edge, edge],
        [pltpu.SemaphoreType.DMA((2,))],
        8000000000,
        movie_r, upstream_r,
        unplaced=(0, 1),
        limit=53.8,
    )
    far = paired(far, 1)
    near = paired(near, 0)
    act_in, pre_part, grad_part = call(
        lambda *refs: inner_kernel(width, *refs),
        [field, part, part],
        [pltpu.VMEM(own_patch.shape, BF16)] * 2,
        3 * conv_flops // 2,
        movie_r, upstream_r, kernel_one, kernel_two,
    )
    keep, send, mid, grad, near_out, far_out = call(
        lambda *refs: outer_kernel(width, *refs),
        [bundle, bundle, field, field, edge, edge],
        [pltpu.VMEM((halo, cells + 2 * width, TAPS * chans), BF16)],
        conv_flops // 2,
        far, near, act_in, upstream_r, pre_part, grad_part, kernel_one, kernel_two,
    )
    other = swapped(send)
    near_mid = paired(near_out, 0)
    far_mid = paired(far_out, 1)

    edge_patch = pltpu.VMEM((halo, cells + 2 * width, TAPS * chans), BF16)

    def middle(mid, grad):
        return call(
            lambda *refs: middle_kernel(width, *refs),
            [part, part],
            [pltpu.VMEM(own_patch.shape, BF16)] * 2,
            3 * conv_flops // 2,
            mid, grad, kernel_one, kernel_two,
        )

    def finish(near_mid, far_mid, out_part, in_part):
        return call(
            lambda *refs: last_kernel(width, *refs),
            [field, field],
            [edge_patch],
            conv_flops // 2,
            movie_r, upstream_r, near_mid, far_mid, out_part, in_part, kernel_one, kernel_two,
        )

    scratch = [
        pltpu.VMEM((ext, cells + 2 * width, TAPS * chans), BF16),
        pltpu.VMEM((chans, ext * cells), BF16),
    ]
    (own_sums,) = call(
        lambda *refs: own_sums_kernel(width, *refs),
        [shape((krows, chans), F32)],
        scratch,
        conv_flops,
        keep,
    )
    if dp == 2 and tm >= 4 and tm & (tm - 1) == 0 and rows % 8 == 0:
        size = tm // 4
        orders = ((1, 2), (2, 1))
        distance = [
            [a * first + b * second + 4 * q for a in range(2) for b in range(2) for q in range(size)]
            for first, second in orders
        ]
        wide, narrow = shape((size, rows, chans), F32), shape((size, rows, chans), BF16)
        stay, pass_on, send_stay, send_on = call(
            lambda *refs: relative_sums_kernel(width, distance, *refs),
            [wide, wide, narrow, narrow],
            [pltpu.VMEM((krows, chans), F32)] + scratch,
            conv_flops,
            own_sums, other,
        )
        send_on, mid, grad = lax.optimization_barrier((send_on, mid, grad))
        parts = middle(mid, grad)
        got_on = exchanged(send_on, (orders[0][0], orders[1][0]))
        got_stay = exchanged(send_stay, (orders[0][0], orders[1][0]))
        got_on, *parts = lax.optimization_barrier((got_on, *parts))
        got = exchanged((pass_on + got_on.astype(F32)).astype(BF16), (orders[0][1], orders[1][1]))
        kept = stay + got_stay.astype(F32) + got.astype(F32)
        gots = [exchanged(kept[q].astype(BF16), (4 * q, 4 * q)) for q in (2, 3, 1)]
        output, movie_grad = finish(near_mid, far_mid, *parts)
        *gots, output, movie_grad = lax.optimization_barrier((*gots, output, movie_grad))
        mine = kept[0]
        for got in gots:
            mine = mine + got.astype(F32)
    else:
        (sums,) = call(
            lambda *refs: plain_sums_kernel(width, *refs),
            [shape((krows, chans), F32)],
            scratch,
            conv_flops,
            own_sums, other,
        )
        output, movie_grad = finish(near_mid, far_mid, *middle(mid, grad))
        mine = lax.psum_scatter(sums, "tm", scatter_dimension=0, tiled=True)
        if dp > 2:
            groups = [[d for d in range(dp) if d % 2 == parity] for parity in range(2)]
            mine = lax.psum(mine, "dp", axis_index_groups=groups)
    theirs = swapped(mine)
    is_even = lax.axis_index("dp") % 2 == 0
    grad_one = jnp.where(is_even, mine, theirs)
    grad_two = jnp.where(is_even, theirs, mine)
    return (output.reshape(movie.shape), movie_grad.reshape(movie.shape), grad_one, grad_two)


def solution(mesh):
    in_specs = (P("dp", "tm", None, None, None), P(), P(), P("dp", "tm", None, None, None))
    out_specs = (
        P("dp", "tm", None, None, None),
        P("dp", "tm", None, None, None),
        P("tm", None),
        P("tm", None),
    )
    return jax.shard_map(body, mesh=mesh, in_specs=in_specs, out_specs=out_specs, check_vma=False)
```

```python
import jax
import jax.numpy as jnp
from jax import lax
from jax.experimental import pallas as pl
from jax.experimental.pallas import tpu as pltpu
from jax.sharding import PartitionSpec as P

BF16 = jnp.bfloat16
F32 = jnp.float32
TAPS = 3


def silu_grad(value):
    sig = jax.nn.sigmoid(value)
    return sig * (1.0 + value * (1.0 - sig))


def fill(patches, first, field, width, mirrored):
    frames, cells, chans = field.shape
    rows = frames * cells
    flat = field.astype(F32).reshape(rows, chans)
    column = lax.broadcasted_iota(jnp.int32, (rows, chans), 0) % width
    before = jnp.where(column == 0, 0.0, pltpu.roll(flat, 1, 0))
    after = jnp.where(column == width - 1, 0.0, pltpu.roll(flat, rows - 1, 0))
    blocks = (after, flat, before) if mirrored else (before, flat, after)
    for k, block in enumerate(blocks):
        patches[pl.ds(first, frames), width : width + cells, k * chans : (k + 1) * chans] = (
            block.astype(BF16).reshape(frames, cells, chans)
        )
    edge = jnp.zeros((frames, width, TAPS * chans), BF16)
    patches[pl.ds(first, frames), :width, :] = edge
    patches[pl.ds(first, frames), width + cells :, :] = edge


def taps_forward(patches, kernel, kt, first, count, cells, width):
    chans = kernel.shape[1]
    left = jnp.concatenate(
        [
            patches[first : first + count, ki * width : ki * width + cells, :].reshape(count * cells, TAPS * chans)
            for ki in range(TAPS)
        ],
        axis=1,
    )
    rows = TAPS * TAPS * chans
    return jnp.dot(left, kernel[kt * rows : (kt + 1) * rows, :], preferred_element_type=F32)


def taps_backward(patches, kernel, kt, first, count, cells, width):
    chans = kernel.shape[1]
    left = jnp.concatenate(
        [
            patches[
                first : first + count, (TAPS - 1 - ki) * width : (TAPS - 1 - ki) * width + cells, :
            ].reshape(count * cells, TAPS * chans)
            for ki in range(TAPS)
        ],
        axis=1,
    )
    taps = range(kt * TAPS * TAPS, (kt + 1) * TAPS * TAPS)
    right = jnp.concatenate([kernel[tap * chans : (tap + 1) * chans, :] for tap in taps], axis=1)
    return lax.dot_general(left, right, (((1,), (1,)), ((), ())), preferred_element_type=F32)


def edges_kernel(movie, upstream, near, far, sems):
    frames = movie.shape[0]
    halo = near.shape[0]
    even = lax.axis_index("tm") % 2 == 0

    def run(forward, backward):
        copies = [
            pltpu.make_async_copy(movie.at[pl.ds(frames - halo, halo)], forward, sems.at[0]),
            pltpu.make_async_copy(upstream.at[pl.ds(0, halo)], backward, sems.at[1]),
        ]
        for copy in copies:
            copy.start()
        for copy in copies:
            copy.wait()

    @pl.when(even)
    def _():
        run(near, far)

    @pl.when(jnp.logical_not(even))
    def _():
        run(far, near)


def sorted_edges(near, far):
    even = lax.axis_index("tm") % 2 == 0
    return jnp.where(even, far[...], near[...]), jnp.where(even, near[...], far[...])


def own_forward(patches, kernel, out, frames, cells, width):
    out[...] = taps_forward(patches, kernel, TAPS - 1, 0, frames, cells, width)
    for lag in range(1, TAPS):
        out[lag * cells :, :] += taps_forward(patches, kernel, TAPS - 1 - lag, 0, frames - lag, cells, width)


def own_backward(patches, kernel, out, frames, cells, width):
    out[...] = taps_backward(patches, kernel, TAPS - 1, 0, frames, cells, width)
    for lag in range(1, TAPS):
        part = taps_backward(patches, kernel, TAPS - 1 - lag, lag, frames - lag, cells, width)
        out[: (frames - lag) * cells, :] += part


def with_before(width, part, patches, kernel, before):
    _, cells, chans = before.shape
    fill(patches, 0, before, width, False)
    sums = [part[row : row + cells, :] for row in range(0, part.shape[0], cells)]
    for kt in range(TAPS - 1):
        count = TAPS - 1 - kt
        more = taps_forward(patches, kernel, kt, kt, count, cells, width)
        for n in range(count):
            sums[n] = sums[n] + more[n * cells : (n + 1) * cells]
    return jnp.concatenate(sums, axis=0)


def with_after(width, part, patches, kernel, after):
    _, cells, chans = after.shape
    fill(patches, 0, after, width, True)
    sums = [part[row : row + cells, :] for row in range(0, part.shape[0], cells)]
    for kt in range(TAPS - 1):
        count = TAPS - 1 - kt
        more = taps_backward(patches, kernel, kt, 0, count, cells, width)
        for n in range(count):
            sums[n - count] = sums[n - count] + more[n * cells : (n + 1) * cells]
    return jnp.concatenate(sums, axis=0)


def inner_kernel(width, movie, upstream, one, two, act_in, pre_part, grad_part, act_patches, up_patches):
    frames, cells, _ = movie.shape
    act_in[...] = jax.nn.silu(movie[...].astype(F32)).astype(BF16)
    fill(act_patches, 0, act_in[...], width, False)
    own_forward(act_patches, one, pre_part, frames, cells, width)
    fill(up_patches, 0, upstream[...], width, True)
    own_backward(up_patches, two, grad_part, frames, cells, width)


def outer_kernel(
    width, far, near, act_in, upstream, pre_part, grad_part, one, two, keep, send, mid, grad, near_out, far_out, patches
):
    frames, cells, chans = act_in.shape
    halo = TAPS - 1
    before, after = sorted_edges(near, far)
    act_before = jax.nn.silu(before.astype(F32)).astype(BF16)
    pre = with_before(width, pre_part, patches, one, act_before)
    act_mid = jax.nn.silu(pre).astype(BF16).reshape(frames, cells, chans)
    mid[...] = act_mid
    mid_grad = with_after(width, grad_part, patches, two, after)
    pre_grad = (mid_grad * silu_grad(pre)).astype(BF16).reshape(frames, cells, chans)
    grad[...] = pre_grad
    even = lax.axis_index("tm") % 2 == 0
    mid_tail, grad_head = act_mid[frames - halo :], pre_grad[:halo]
    near_out[...] = jnp.where(even, mid_tail, grad_head)
    far_out[...] = jnp.where(even, grad_head, mid_tail)

    def store(for_one, for_two):
        for_one[:frames] = grad[...]
        for_one[frames : frames + halo] = act_before
        for_one[frames + halo :] = act_in[...]
        for_two[:frames] = mid[...]
        for_two[frames : 2 * frames] = upstream[...]
        for_two[2 * frames :] = after

    is_even = lax.axis_index("dp") % 2 == 0

    @pl.when(is_even)
    def _():
        store(keep, send)

    @pl.when(jnp.logical_not(is_even))
    def _():
        store(send, keep)


def kernel_sums(width, source, acc, patches, turned, before=None):
    ext_frames, cells, chans = source.shape
    halo = TAPS - 1
    frames = (ext_frames - halo) // 2
    odd = lax.axis_index("dp") % 2
    fill(patches, 0, source[pl.ds(odd * frames, frames + halo)], width, True)
    for n in range(frames + halo):
        turned[:, n * cells : (n + 1) * cells] = source[(1 - odd) * frames + n].T
    for kt in range(TAPS):
        l_start = (1 - odd) * kt
        r_start = odd * (halo - kt)
        left = turned[:, pl.ds(pl.multiple_of(l_start * cells, cells), frames * cells)]
        for ki in range(TAPS):
            low = (halo - ki) * width
            right = patches[pl.ds(r_start, frames), low : low + cells, :].reshape(frames * cells, TAPS * chans)
            sums = jnp.dot(left, right, preferred_element_type=F32)
            for kj in range(TAPS):
                row = ((kt * TAPS + ki) * TAPS + kj) * chans
                part = sums[:, kj * chans : (kj + 1) * chans]
                if before is not None:
                    part = part + before[row : row + chans, :]
                acc[row : row + chans, :] = part


def own_sums_kernel(width, own, acc, patches, turned):
    kernel_sums(width, own, acc, patches, turned)


def plain_sums_kernel(width, own_sums, other, acc, patches, turned):
    kernel_sums(width, other, acc, patches, turned, own_sums)


def pick_blocks(acc, quarter, distance, first):
    size, rows, _ = quarter.shape
    odd = lax.axis_index("dp") % 2
    me = lax.axis_index("tm")
    for r in range(size):
        far = jnp.where(odd == 1, distance[1][first + r], distance[0][first + r])
        block = jnp.bitwise_xor(me, far)
        part = acc[pl.ds(pl.multiple_of(block * rows, 8), rows), :]
        quarter[r] = part.astype(quarter.dtype)


def relative_sums_kernel(width, distance, own_sums, other, acc, send_on, patches, turned):
    kernel_sums(width, other, acc, patches, turned, own_sums)
    pick_blocks(acc, send_on, distance, 3 * send_on.shape[0])


def rest_kernel(distance, acc, stay, pass_on, send_stay):
    for n, quarter in enumerate((stay, pass_on, send_stay)):
        pick_blocks(acc, quarter, distance, n * quarter.shape[0])


def middle_kernel(width, mid, grad, one, two, out_part, in_part, mid_patches, grad_patches):
    frames, cells, _ = mid.shape
    fill(mid_patches, 0, mid[...], width, False)
    own_forward(mid_patches, two, out_part, frames, cells, width)
    fill(grad_patches, 0, grad[...], width, True)
    own_backward(grad_patches, one, in_part, frames, cells, width)


def last_kernel(width, movie, upstream, near, far, out_part, in_part, one, two, output, movie_grad, patches):
    shape = movie.shape
    mid_before, grad_after = sorted_edges(near, far)
    movie_f = movie[...].astype(F32)
    out = with_before(width, out_part, patches, two, mid_before).reshape(shape)
    output[...] = (movie_f + out).astype(BF16)
    in_grad = with_after(width, in_part, patches, one, grad_after).reshape(shape)
    movie_grad[...] = (upstream[...].astype(F32) + in_grad * silu_grad(movie_f)).astype(BF16)


def call(body, outs, scratch, flops, *args, unplaced=(), limit=24):
    vmem = pl.BlockSpec(memory_space=pltpu.VMEM)
    anywhere = pl.BlockSpec(memory_space=pltpu.MemorySpace.HBM)
    size = sum(a.size * a.dtype.itemsize for a in args) + sum(o.size * o.dtype.itemsize for o in outs)
    return pl.pallas_call(
        body,
        out_shape=outs,
        in_specs=[anywhere if i in unplaced else vmem for i in range(len(args))],
        out_specs=[vmem] * len(outs),
        scratch_shapes=scratch,
        compiler_params=pltpu.CompilerParams(vmem_limit_bytes=int(limit * 2**20)),
        cost_estimate=pl.CostEstimate(flops=flops, bytes_accessed=size, transcendentals=0),
    )(*args)


def paired(block, first):
    pairs = [(i, i + 1) for i in range(first, lax.axis_size("tm") - 1, 2)]
    return lax.ppermute(block, "tm", pairs + [(j, i) for i, j in pairs])


def swapped(block):
    return lax.ppermute(block, "dp", [(i, i ^ 1) for i in range(lax.axis_size("dp"))])


def exchanged(send, steps):
    tm, dp = lax.axis_size("tm"), lax.axis_size("dp")
    route = [(t * dp + d, (t ^ steps[d % 2]) * dp + d) for t in range(tm) for d in range(dp)]
    return lax.ppermute(send, ("tm", "dp"), route)


def body(movie, kernel_one, kernel_two, upstream):
    clips, frames, height, width, chans = movie.shape
    assert clips == 1
    tm, dp = lax.axis_size("tm"), lax.axis_size("dp")
    assert dp % 2 == 0
    cells = height * width
    halo = TAPS - 1
    ext = frames + halo
    krows = kernel_one.shape[0]
    rows = krows // tm
    shape = jax.ShapeDtypeStruct
    flat = (frames, cells, chans)
    movie_r = movie.reshape(flat)
    upstream_r = upstream.reshape(flat)
    conv_flops = 2 * frames * cells * krows * chans

    bundle = shape((frames + ext, cells, chans), BF16)
    field = shape(flat, BF16)
    edge = shape((halo, cells, chans), BF16)
    part = shape((frames * cells, chans), F32)
    own_patch = shape((frames, cells + 2 * width, TAPS * chans), BF16)

    near, far = call(
        edges_kernel,
        [edge, edge],
        [pltpu.SemaphoreType.DMA((2,))],
        8000000000,
        movie_r, upstream_r,
        unplaced=(0, 1),
        limit=53.8,
    )
    far = paired(far, 1)
    near = paired(near, 0)
    act_in, pre_part, grad_part = call(
        lambda *refs: inner_kernel(width, *refs),
        [field, part, part],
        [pltpu.VMEM(own_patch.shape, BF16)] * 2,
        3 * conv_flops // 2,
        movie_r, upstream_r, kernel_one, kernel_two,
    )
    keep, send, mid, grad, near_out, far_out = call(
        lambda *refs: outer_kernel(width, *refs),
        [bundle, bundle, field, field, edge, edge],
        [pltpu.VMEM((halo, cells + 2 * width, TAPS * chans), BF16)],
        conv_flops // 2,
        far, near, act_in, upstream_r, pre_part, grad_part, kernel_one, kernel_two,
    )
    other = swapped(send)
    near_mid = paired(near_out, 0)
    far_mid = paired(far_out, 1)

    edge_patch = pltpu.VMEM((halo, cells + 2 * width, TAPS * chans), BF16)

    def middle(mid, grad):
        return call(
            lambda *refs: middle_kernel(width, *refs),
            [part, part],
            [pltpu.VMEM(own_patch.shape, BF16)] * 2,
            3 * conv_flops // 2,
            mid, grad, kernel_one, kernel_two,
        )

    def finish(near_mid, far_mid, out_part, in_part):
        return call(
            lambda *refs: last_kernel(width, *refs),
            [field, field],
            [edge_patch],
            conv_flops // 2,
            movie_r, upstream_r, near_mid, far_mid, out_part, in_part, kernel_one, kernel_two,
        )

    scratch = [
        pltpu.VMEM((ext, cells + 2 * width, TAPS * chans), BF16),
        pltpu.VMEM((chans, ext * cells), BF16),
    ]
    (own_sums,) = call(
        lambda *refs: own_sums_kernel(width, *refs),
        [shape((krows, chans), F32)],
        scratch,
        conv_flops,
        keep,
    )
    if dp == 2 and tm >= 4 and tm & (tm - 1) == 0 and rows % 8 == 0:
        size = tm // 4
        orders = ((1, 2), (2, 1))
        distance = [
            [a * first + b * second + 4 * q for a in range(2) for b in range(2) for q in range(size)]
            for first, second in orders
        ]
        wide, narrow = shape((size, rows, chans), F32), shape((size, rows, chans), BF16)
        sums, send_on = call(
            lambda *refs: relative_sums_kernel(width, distance, *refs),
            [shape((krows, chans), F32), narrow],
            scratch,
            conv_flops,
            own_sums, other,
        )
        stay, pass_on, send_stay = call(
            lambda *refs: rest_kernel(distance, *refs), [wide, wide, narrow], [], conv_flops // 4, sums
        )
        send_on, mid, grad = lax.optimization_barrier((send_on, mid, grad))
        parts = middle(mid, grad)
        got_on = exchanged(send_on, (orders[0][0], orders[1][0]))
        got_stay = exchanged(send_stay, (orders[0][0], orders[1][0]))
        got_on, *parts = lax.optimization_barrier((got_on, *parts))
        got = exchanged((pass_on + got_on.astype(F32)).astype(BF16), (orders[0][1], orders[1][1]))
        kept = stay + got_stay.astype(F32) + got.astype(F32)
        gots = [exchanged(kept[q].astype(BF16), (4 * q, 4 * q)) for q in (2, 3, 1)]
        output, movie_grad = finish(near_mid, far_mid, *parts)
        *gots, output, movie_grad = lax.optimization_barrier((*gots, output, movie_grad))
        mine = kept[0]
        for got in gots:
            mine = mine + got.astype(F32)
    else:
        (sums,) = call(
            lambda *refs: plain_sums_kernel(width, *refs),
            [shape((krows, chans), F32)],
            scratch,
            conv_flops,
            own_sums, other,
        )
        output, movie_grad = finish(near_mid, far_mid, *middle(mid, grad))
        mine = lax.psum_scatter(sums, "tm", scatter_dimension=0, tiled=True)
        if dp > 2:
            groups = [[d for d in range(dp) if d % 2 == parity] for parity in range(2)]
            mine = lax.psum(mine, "dp", axis_index_groups=groups)
    theirs = swapped(mine)
    is_even = lax.axis_index("dp") % 2 == 0
    grad_one = jnp.where(is_even, mine, theirs)
    grad_two = jnp.where(is_even, theirs, mine)
    return (output.reshape(movie.shape), movie_grad.reshape(movie.shape), grad_one, grad_two)


def solution(mesh):
    in_specs = (P("dp", "tm", None, None, None), P(), P(), P("dp", "tm", None, None, None))
    out_specs = (
        P("dp", "tm", None, None, None),
        P("dp", "tm", None, None, None),
        P("tm", None),
        P("tm", None),
    )
    return jax.shard_map(body, mesh=mesh, in_specs=in_specs, out_specs=out_specs, check_vma=False)
```
